128 devices in a mesh: comp: 2 (over z_lo), gx: 8 (over x, core), gy: 8 (over y, z_hi).
Axes of the slice: x: 4, y: 4, z: 4 (z_hi: 2, z_lo: 2; z = z_hi * 2 + z_lo), core: 2. Of those that a mesh axis runs over, the one named last changes fastest.
Arguments:
- state: float32 [2, 16, 1024, 1024], P('comp', None, 'gx', 'gy'), may hold values from -6 to 6
- velocity: bfloat16 [2, 2, 16, 1024, 1024], P('comp', None, None, 'gx', 'gy'), may hold values from -0.5 to 0.5
- diffusivity: float32 [2, 16], P('comp'), may hold values from 0.02 to 0.2
- export_proj: float32 [2, 8, 16], P('comp'), may hold values from -1.5 to 1.5
- import_proj: float32 [2, 16, 8], P('comp'), may hold values from -2 to 2
- intersection_weights: bfloat16 [2, 1024, 8, 4, 128, 128], P('comp', 'gx', 'gy'), may hold values from -0.25 to 0.25
- recv_slots: int32 [2, 1024, 8, 4], P('comp', 'gx', 'gy'), may hold values from 0 to 1023, as said below
- send_slots: int32 [2, 8, 8, 64, 16], P(None, 'gx', 'gy'), may hold values from 0 to 127, as said below
- land: int32 [1024, 8], P('gx', 'gy'), may hold values 0 or 1
Outputs:
- new_state: float32 [2, 16, 1024, 1024], P('comp', None, 'gx', 'gy')
- imported: bfloat16 [2, 1024, 8, 1024], P('comp', 'gx', None, 'gy')
The draws below stay inside these ranges and needn't reach their ends.
Inputs may be any that keep to these rules, and one draw needn't show every extreme that they name: `recv_slots`: entry p names the place, source device times 16 plus place, in the buffer from the other component; each destination device reads each place at most once; at most 16 of one destination device's tiles' references come from one source device, and for every destination device exactly 16 come from one source device. Source devices are numbered row-major over gx and gy. `send_slots`: entry [c, a, b, d, q] is the local block row that source device (a, b) of component c puts into place q of its buffer for destination device d of the other component; places that no destination reads hold 0.
All inputs are finite; a program needn't handle non-finite values. No bound on the sum of `land` on one device may be relied on, other than what follows from the above.
Results may differ from the reference program's by a relative error of at most 0.0049.
Values may be sent and summed in bfloat16 or wider, within the bound.
A program may use at most 128 MiB of HBM per device.

```python
import math
import jax
import jax.numpy as jnp
from jax import lax

LEV = 16
CX = 128
TILE = 128
FLD = 8
K = 4
STEPS = 2
ROWS = 1024
COLS = 1024
GROUP = 64
CAP = 16
N_GX = 8
N_GY = 8


def intersection_tables(key):
    base_key = jax.random.fold_in(key, 7)
    slots_total = GROUP * CAP
    ref_count = CX * K
    sub_keys = jax.random.split(base_key, 2 * GROUP)

    def draw_one(sub_key):
        key_full, key_perm, key_refs, key_tiles = jax.random.split(sub_key, 4)
        full_source = jax.random.randint(key_full, (), 0, GROUP)
        shuffled = jax.random.permutation(key_perm, slots_total).astype(jnp.int32)
        rank_of = jnp.argsort(shuffled).astype(jnp.int32)
        places = jnp.arange(slots_total, dtype=jnp.int32)
        priority = jnp.where(places // CAP == full_source, places - slots_total, rank_of)
        ordered = jnp.argsort(priority).astype(jnp.int32)
        used_slots = ordered[:ref_count]
        picked = used_slots[jax.random.permutation(key_refs, ref_count)]
        used_marks = jnp.zeros((slots_total,), jnp.int32).at[used_slots].set(1)
        tile_rows = jax.random.randint(key_tiles, (slots_total,), 0, CX) * used_marks
        return (picked, tile_rows)
    picked, tile_rows = jax.vmap(draw_one)(sub_keys)
    recv_table = picked.reshape(2, N_GX, N_GY, CX, K).transpose(0, 1, 3, 2, 4).reshape(2, ROWS, N_GY, K)
    send_table = tile_rows.reshape(2, GROUP, GROUP, CAP).transpose(0, 2, 1, 3)[::-1].reshape(2, N_GX, N_GY, GROUP, CAP)
    return (recv_table.astype(jnp.int32), send_table.astype(jnp.int32))


def draw_recv_slots(key, part):
    return intersection_tables(key)[0]


def draw_send_slots(key, part):
    return intersection_tables(key)[1]


def plant(result, key, least, high):
    longest = result.shape.index(max(result.shape))
    spots = []
    for shift in (0, 1):
        where = [jax.random.randint(jax.random.fold_in(key, axis), (), 0, length) for axis, length in enumerate(result.shape)]
        where[longest] = (where[longest] + shift) % result.shape[longest]
        spots.append(tuple(where))
    return result.at[spots[0]].set(least).at[spots[1]].set(high)


def steps_of(key, shape, cuts, smallest, high):
    gain = 1.0
    for position, parts in cuts:
        draws = jax.random.uniform(jax.random.fold_in(jax.random.fold_in(key, 6), position), (parts,), jnp.float32, smallest / len(cuts), high / len(cuts))
        gain = gain * jnp.repeat(jnp.exp(draws), shape[position] // parts).reshape((-1,) + (1,) * (len(shape) - 1 - position))
    return gain


def gaussian(key, dims, width, reach, shards=(), held_as=jnp.bfloat16):
    array = jax.random.normal(key, dims, jnp.float32) * width
    if len(shards) > 0:
        array = steps_of(key, dims, shards, -0.22, 0.18) * array
    return jnp.clip(array, min=-reach, max=reach).astype(held_as)


def setup_inputs(seed: int = 0) -> dict:
    key_list = jax.random.split(jax.random.key(seed), 10)
    return {
        "state": gaussian(key_list[0], (2, LEV, ROWS, COLS), 1.0, 6.0, ((0, 2), (2, 8), (3, 8)), jnp.float32),
        "velocity": jnp.clip(jax.random.uniform(key_list[1], (2, 2, LEV, ROWS, COLS), jnp.float32, -0.5, 0.5) * steps_of(key_list[1], (2, 2, LEV, ROWS, COLS), ((0, 2), (3, 8), (4, 8)), -0.4, 0.0), -0.5, 0.5).astype(jnp.bfloat16),
        "diffusivity": jnp.clip(jnp.exp(math.log(0.2) - 2.3025851 * jax.random.uniform(key_list[2], (2, LEV), jnp.float32) ** steps_of(key_list[2], (2, LEV), ((0, 2),), -0.2, 0.2)), 0.02, 0.2),
        "export_proj": gaussian(key_list[3], (2, FLD, LEV), LEV ** -0.5, 1.5, ((0, 2),), jnp.float32),
        "import_proj": gaussian(key_list[4], (2, LEV, FLD), FLD ** -0.5, 2.0, ((0, 2),), jnp.float32),
        "intersection_weights": gaussian(key_list[5], (2, ROWS, N_GY, K, TILE, TILE), (K * TILE) ** -0.5, 0.25, ((0, 2), (1, 8), (2, 8))),
        "recv_slots": draw_recv_slots(jax.random.fold_in(key_list[9], 71), 0),
        "send_slots": draw_send_slots(jax.random.fold_in(key_list[9], 71), 0),
        "land": plant((jax.random.randint(key_list[8], (ROWS, N_GY), 0, 10) < 7).astype(jnp.int32), jax.random.fold_in(key_list[8], 1), 0, 1),
    }


def advance(tracer, speeds, coeffs, wet_mask):
    padded = jnp.pad(tracer, ((0, 0), (1, 1), (1, 1)))
    row_down = padded[:, 2:, 1:-1]
    row_up = padded[:, :-2, 1:-1]
    col_right = padded[:, 1:-1, 2:]
    col_left = padded[:, 1:-1, :-2]
    spread = row_down + row_up + col_right + col_left - 4.0 * tracer
    carried = 0.5 * (speeds[0].astype(jnp.float32) * (row_down - row_up) + speeds[1].astype(jnp.float32) * (col_right - col_left))
    return tracer + wet_mask * (coeffs[:, None, None] * spread - carried)


def reference(state, velocity, diffusivity, export_proj, import_proj, intersection_weights, recv_slots, send_slots, land):
    highest = lax.Precision.HIGHEST
    wet_ocean = jnp.repeat(land.astype(jnp.float32), TILE, axis=1)
    wet_cells = jnp.stack([jnp.ones_like(wet_ocean), wet_ocean])
    wet_tiles = jnp.stack([jnp.ones(land.shape, jnp.float32), land.astype(jnp.float32)])
    exported = (jnp.einsum("cfl,clxy->cfxy", export_proj, state, precision=highest) * wet_cells[:, None]).astype(jnp.bfloat16)
    tile_set = exported.reshape(2, FLD, N_GX, CX, N_GY, TILE).transpose(0, 2, 4, 3, 1, 5).reshape(2, GROUP * CX, FLD, TILE)
    send_flat = send_slots.reshape(2, GROUP, GROUP, CAP)
    dest_dev = (jnp.arange(ROWS, dtype=jnp.int32)[:, None] // CX) * N_GY + jnp.arange(N_GY, dtype=jnp.int32)[None, :]
    source_dev = (recv_slots // CAP).astype(jnp.int32)
    source_place = (recv_slots % CAP).astype(jnp.int32)
    source_comp = (1 - jnp.arange(2, dtype=jnp.int32))[:, None, None, None]
    local_row = send_flat[source_comp, source_dev, dest_dev[None, :, :, None], source_place]
    gathered = tile_set[source_comp, (source_dev * CX + local_row).astype(jnp.int32)]

    def one_row(pair):
        pieces, weights = pair
        return jnp.einsum("bkfm,bkom->bfo", pieces.astype(jnp.float32), weights.astype(jnp.float32), precision=highest)

    summed = lax.map(one_row, (gathered.reshape(2 * ROWS, N_GY, K, FLD, TILE), intersection_weights.reshape(2 * ROWS, N_GY, K, TILE, TILE)))
    summed = summed.reshape(2, ROWS, N_GY, FLD, TILE) * wet_tiles[:, :, :, None, None]
    imported = summed.astype(jnp.bfloat16).transpose(0, 1, 3, 2, 4).reshape(2, ROWS, FLD, COLS)
    results = []
    for section in range(2):
        tracer = state[section]
        for repeat in range(STEPS):
            tracer = advance(tracer, velocity[section], diffusivity[section], wet_cells[section])
        forcing = jnp.einsum("lf,xfy->lxy", import_proj[section], imported[section].astype(jnp.float32), precision=highest)
        results.append(tracer + wet_cells[section] * forcing)
    return jnp.stack(results), imported
```

```python
import functools

import jax
import jax.numpy as jnp
from jax import lax
from jax.experimental import pallas as pl
from jax.experimental.pallas import tpu as pltpu
from jax.sharding import PartitionSpec as P

MESH = pl.DeviceIdType.MESH
F32 = jnp.float32
BF16 = jnp.bfloat16

LEV, FLD, K = 16, 8, 4
ROWS, TILE = 128, 128
N_GX, N_GY = 8, 8
GROUP, CAP = 64, 16
TOP = 8
PADDED = ROWS + 2 * TOP
W_PARTS = 8
FIRST, SECOND = 12, 44


def partner(turn, gx, gy):
    x = lax.rem(lax.div(gx, 2) + lax.div(turn, 16), 4)
    core = lax.rem(lax.rem(gx, 2) + lax.rem(lax.div(turn, 8), 2), 2)
    y = lax.rem(lax.div(gy, 2) + lax.rem(lax.div(turn, 2), 4), 4)
    high = lax.rem(lax.rem(gy, 2) + lax.rem(turn, 2), 2)
    return x * 2 + core, y * 2 + high


def exchange_kernel(
    state_hbm, vel_hbm, w_hbm, proj, diff, table, land, land_row,
    arrived, tracer, w_out,
    ta, tb, vel, ex, buf, halo_out, halo_in, wet,
    sem_state, sem_vel, sem_w, sem_send, sem_recv, sem_hs, sem_hr,
):
    comp, gx, gy = lax.axis_index("comp"), lax.axis_index("gx"), lax.axis_index("gy")
    other = 1 - comp
    me = gx * N_GY + gy
    up, down = lax.rem(gx + N_GX - 1, N_GX), lax.rem(gx + 1, N_GX)
    left, right = lax.rem(gy + N_GY - 1, N_GY), lax.rem(gy + 1, N_GY)
    beside = ((comp, up, gy), (comp, down, gy), (comp, gx, left), (comp, gx, right))

    interior = pl.ds(TOP, ROWS)
    get_state = pltpu.make_async_copy(state_hbm, ta.at[:, interior], sem_state)
    get_state.start()
    get_vel = pltpu.make_async_copy(vel_hbm, vel, sem_vel)
    get_vel.start()

    barrier = pltpu.get_barrier_semaphore()
    for device in beside:
        pl.semaphore_signal(barrier, inc=1, device_id=device, device_id_type=MESH)

    def greet(d, carry):
        pl.semaphore_signal(
            barrier, inc=1, device_id=(other, lax.div(d, N_GY), lax.rem(d, N_GY)), device_id_type=MESH
        )
        return carry

    lax.fori_loop(0, GROUP, greet, 0)

    part = w_hbm.shape[0] // W_PARTS

    def get_w(i):
        rows = pl.ds(i * part, part)
        return pltpu.make_async_copy(w_hbm.at[rows], w_out.at[rows], sem_w.at[i])

    for i in range(W_PARTS):
        get_w(i).start()

    row_wet = jnp.where(comp == 0, jnp.ones((1, TILE), F32), land_row[...].astype(F32))
    wet[...] = jnp.transpose(jnp.broadcast_to(row_wet, (ROWS, TILE)))

    columns = [jnp.broadcast_to(proj[:, l : l + 1], (FLD, TILE)) for l in range(LEV)]
    get_state.wait()

    def export(i, carry):
        for j in range(4):
            x = i * 4 + j
            total = columns[0] * ta[0, pl.ds(TOP + x, 1), :]
            for l in range(1, LEV):
                total += columns[l] * ta[l, pl.ds(TOP + x, 1), :]
            ex[x] = total * jnp.where(comp == 0, 1.0, land[0, x].astype(F32))
        return carry

    lax.fori_loop(0, ROWS // 4, export, 0)
    pl.semaphore_wait(barrier, GROUP + 4)

    def serve(turn, carry):
        to_x, to_y = partner(turn, gx, gy)
        d = to_x * N_GY + to_y
        for q in range(CAP):
            buf[turn * CAP + q] = ex[table[comp, q, d]].astype(BF16)
        pltpu.make_async_remote_copy(
            src_ref=buf.at[pl.ds(turn * CAP, CAP)],
            dst_ref=arrived.at[pl.ds(me * CAP, CAP)],
            send_sem=sem_send,
            recv_sem=sem_recv,
            device_id=(other, to_x, to_y),
            device_id_type=MESH,
        ).start()
        return carry

    def pick(l):
        r = lax.broadcasted_iota(jnp.int32, (2 * LEV, TILE), 0)
        c = lax.broadcasted_iota(jnp.int32, (2 * LEV, TILE), 1)
        hit = ((r == l) & (c == 0)) | ((r == LEV + l) & (c == TILE - 1))
        return jnp.where(hit, 1.0, 0.0).astype(BF16)

    def halo_copy(turn, side):
        return pltpu.make_async_remote_copy(
            src_ref=halo_out.at[turn, side],
            dst_ref=halo_in.at[turn, side],
            send_sem=sem_hs.at[turn, side],
            recv_sem=sem_hr.at[turn, side],
            device_id=beside[side],
            device_id_type=MESH,
        )

    def send_halo(turn, t):
        flat = t.reshape(LEV * PADDED, TILE)
        halo_out[turn, 0] = flat[pl.ds(TOP, LEV, stride=PADDED), :].astype(BF16)
        halo_out[turn, 1] = flat[pl.ds(TOP + ROWS - 1, LEV, stride=PADDED), :].astype(BF16)

        def add(l, total):
            return total + lax.dot_general(
                pick(l), t[l, interior, :].astype(BF16), (((1,), (1,)), ((), ())), preferred_element_type=F32
            )

        edges = lax.fori_loop(0, LEV, add, jnp.zeros((2 * LEV, TILE), F32)).astype(BF16)
        halo_out[turn, 2] = edges[:LEV]
        halo_out[turn, 3] = edges[LEV:]
        for side in range(4):
            halo_copy(turn, side).start()

    def take_halo(turn, t):
        for side in range(4):
            halo_copy(turn, side).wait_recv()
        flat = t.reshape(LEV * PADDED, TILE)
        rows = [halo_in[turn, side].astype(F32) for side in range(4)]
        flat[pl.ds(TOP + ROWS, LEV, stride=PADDED), :] = jnp.where(gx < N_GX - 1, rows[0], 0.0)
        flat[pl.ds(TOP - 1, LEV, stride=PADDED), :] = jnp.where(gx > 0, rows[1], 0.0)
        last = jnp.where(gy < N_GY - 1, rows[2], 0.0)
        first = jnp.where(gy > 0, rows[3], 0.0)
        return jnp.transpose(jnp.concatenate([first, last], axis=0)).astype(BF16)

    def advance(t, edges, put):
        lane = lax.broadcasted_iota(jnp.int32, (ROWS, TILE), 1)

        def level(l, carry):
            mid = t[l, interior, :]
            above, below = t[l, pl.ds(TOP - 1, ROWS), :], t[l, pl.ds(TOP + 1, ROWS), :]
            sides = jnp.dot(edges, pick(l), preferred_element_type=F32)
            before = jnp.where(lane == 0, sides, pltpu.roll(mid, 1, 1))
            after = jnp.where(lane == TILE - 1, sides, pltpu.roll(mid, TILE - 1, 1))
            spread = above + below + before + after - 4.0 * mid
            carried = 0.5 * (
                vel[0, l].astype(F32) * (below - above) + vel[1, l].astype(F32) * (after - before)
            )
            put(l, mid + wet[...] * (diff[0, l] * spread - carried))
            return carry

        lax.fori_loop(0, LEV, level, 0)

    def put_tb(l, value):
        tb[l, interior, :] = value

    def put_tracer(l, value):
        tracer[l] = value

    lax.fori_loop(0, FIRST, serve, 0)
    send_halo(0, ta)
    lax.fori_loop(FIRST, SECOND, serve, 0)
    edges = take_halo(0, ta)
    get_vel.wait()
    advance(ta, edges, put_tb)
    send_halo(1, tb)
    lax.fori_loop(SECOND, GROUP, serve, 0)
    edges = take_halo(1, tb)
    advance(tb, edges, put_tracer)

    for i in range(W_PARTS):
        get_w(i).wait()
    for turn in range(2):
        for side in range(4):
            halo_copy(turn, side).wait_send()
    pltpu.make_async_copy(buf, buf, sem_send).wait()
    pltpu.make_async_copy(arrived, arrived, sem_recv).wait()


def remap_kernel(chunk, recv, land, ip, w, arrived, tracer, new_hbm, imp_hbm, new, imp, spread, sem_out):
    comp = lax.axis_index("comp")

    def out_copies(i):
        rows = pl.ds(pl.multiple_of(i * chunk, chunk), chunk)
        return (
            pltpu.make_async_copy(new.at[:, rows], new_hbm.at[:, rows], sem_out.at[0, i]),
            pltpu.make_async_copy(imp.at[rows], imp_hbm.at[rows], sem_out.at[1, i]),
        )

    for f in range(FLD):
        for l in range(LEV):
            spread[f, l : l + 1, :] = jnp.full((1, TILE), ip[f, l], F32)
    tracer_rows = tracer.reshape(LEV * ROWS, TILE)
    new_rows = new.reshape(LEV * ROWS, TILE)

    def step(i, carry):
        for j in range(chunk):
            x = i * chunk + j
            wet = jnp.where(comp == 0, 1.0, land[0, x].astype(F32))
            source = jnp.concatenate([arrived[recv[k, x]] for k in range(K)], axis=1)
            weights = jnp.concatenate([w[x, k] for k in range(K)], axis=1)
            summed = lax.dot_general(source, weights, (((1,), (1,)), ((), ())), preferred_element_type=F32)
            got = (summed * wet).astype(BF16)
            imp[x] = got
            got = got.astype(F32)
            force = spread[0] * got[0:1, :]
            for f in range(1, FLD):
                force += spread[f] * got[f : f + 1, :]
            rows = pl.ds(x, LEV, stride=ROWS)
            new_rows[rows, :] = tracer_rows[rows, :] + wet * force
        for copy in out_copies(i):
            copy.start()
        return carry

    def drain(i, carry):
        for copy in out_copies(i):
            copy.wait()
        return carry

    lax.fori_loop(0, ROWS // chunk, step, 0)
    lax.fori_loop(0, ROWS // chunk, drain, 0)


ANY = pl.BlockSpec(memory_space=pl.ANY)
HBM = pl.BlockSpec(memory_space=pltpu.HBM)
VMEM = pl.BlockSpec(memory_space=pltpu.VMEM)
SMEM = pl.BlockSpec(memory_space=pltpu.SMEM)


def exchange(state, velocity, weights, proj, diff, table, land):
    dma = pltpu.SemaphoreType.DMA
    return pl.pallas_call(
        exchange_kernel,
        name="exchange",
        out_shape=(
            pltpu.VMEM((GROUP * CAP, FLD, TILE), BF16),
            pltpu.VMEM((LEV, ROWS, TILE), F32),
            pltpu.VMEM((ROWS, K, TILE, TILE), BF16),
        ),
        in_specs=[HBM, HBM, HBM, VMEM, SMEM, SMEM, SMEM, VMEM],
        out_specs=(VMEM, VMEM, VMEM),
        scratch_shapes=[
            pltpu.VMEM((LEV, PADDED, TILE), F32),
            pltpu.VMEM((LEV, PADDED, TILE), F32),
            pltpu.VMEM((2, LEV, ROWS, TILE), BF16),
            pltpu.VMEM((ROWS, FLD, TILE), F32),
            pltpu.VMEM((GROUP * CAP, FLD, TILE), BF16),
            pltpu.VMEM((2, 4, LEV, TILE), BF16),
            pltpu.VMEM((2, 4, LEV, TILE), BF16),
            pltpu.VMEM((ROWS, TILE), F32),
            dma,
            dma,
            dma((W_PARTS,)),
            dma,
            dma,
            dma((2, 4)),
            dma((2, 4)),
        ],
        compiler_params=pltpu.CompilerParams(collective_id=0, has_side_effects=True, vmem_limit_bytes=16 << 20),
    )(*(pltpu.with_memory_space_constraint(a, pltpu.HBM) for a in (state, velocity, weights)), proj, diff, table, land, land)


def remap(recv, land, import_proj, weights, arrived, tracer):
    chunk = 16
    return pl.pallas_call(
        functools.partial(remap_kernel, chunk),
        name="remap",
        out_shape=(
            jax.ShapeDtypeStruct((LEV, ROWS, TILE), F32),
            jax.ShapeDtypeStruct((ROWS, FLD, TILE), BF16),
        ),
        in_specs=[SMEM, SMEM, SMEM, VMEM, VMEM, VMEM],
        out_specs=(ANY, ANY),
        scratch_shapes=[
            pltpu.VMEM((LEV, ROWS, TILE), F32),
            pltpu.VMEM((ROWS, FLD, TILE), BF16),
            pltpu.VMEM((FLD, LEV, TILE), F32),
            pltpu.SemaphoreType.DMA((2, ROWS // chunk)),
        ],
        compiler_params=pltpu.CompilerParams(vmem_limit_bytes=16 << 20),
    )(recv, land, import_proj, *(pltpu.with_memory_space_constraint(a, pltpu.VMEM) for a in (weights, arrived, tracer)))


def per_device(
    state, velocity, diffusivity, export_proj, import_proj, intersection_weights, recv_slots, send_slots, land
):
    land = land.reshape(1, ROWS)
    table = send_slots[:, 0, 0].transpose(0, 2, 1)
    recv = recv_slots[0, :, 0].T
    arrived, tracer, weights = exchange(
        state[0], velocity[0], intersection_weights[0, :, 0], export_proj[0], diffusivity, table, land
    )
    new_state, imported = remap(recv, land, import_proj[0].T, weights, arrived, tracer)
    return new_state[None], imported[None]


def solution(mesh):
    return jax.shard_map(
        per_device,
        mesh=mesh,
        in_specs=(
            P("comp", None, "gx", "gy"),
            P("comp", None, None, "gx", "gy"),
            P("comp", None),
            P("comp", None, None),
            P("comp", None, None),
            P("comp", "gx", "gy", None, None, None),
            P("comp", "gx", "gy", None),
            P(None, "gx", "gy", None, None),
            P("gx", "gy"),
        ),
        out_specs=(P("comp", None, "gx", "gy"), P("comp", "gx", None, "gy")),
        check_vma=False,
    )
```

```python
import functools

import jax
import jax.numpy as jnp
from jax import lax
from jax.experimental import pallas as pl
from jax.experimental.pallas import tpu as pltpu
from jax.sharding import PartitionSpec as P

MESH = pl.DeviceIdType.MESH
F32 = jnp.float32
BF16 = jnp.bfloat16

LEV, FLD, K = 16, 8, 4
ROWS, TILE = 128, 128
N_GX, N_GY = 8, 8
GROUP, CAP = 64, 16
TOP = 8
PADDED = ROWS + 2 * TOP
W_PARTS = 8
FIRST, SECOND = 16, 48


def partner(turn, gx, gy):
    block, i = lax.div(turn, 16), lax.rem(turn, 16)
    step_x = lax.rem(i, 4)
    step_y = lax.rem(lax.div(i, 4) + i, 4)
    step_high = lax.rem(i + block, 2)
    step_core = lax.div(block, 2)
    x = lax.rem(lax.div(gx, 2) + step_x, 4)
    core = lax.rem(gx + step_core, 2)
    y = lax.rem(lax.div(gy, 2) + step_y, 4)
    high = lax.rem(gy + step_high, 2)
    return x * 2 + core, y * 2 + high


def exchange_kernel(
    state_hbm, vel_hbm, w_hbm, proj_hbm, diff_hbm, table_hbm, land_hbm, recv_hbm, ip_hbm,
    arrived, tracer, w_out, spread, recv_out, land_out,
    ta, tb, vel, ex, buf, halo_out, halo_in, edge, wet, proj, land_row, diff, table, ip,
    sem_state, sem_vel, sem_small, sem_w, sem_send, sem_recv, sem_hs, sem_hr,
):
    comp, gx, gy = lax.axis_index("comp"), lax.axis_index("gx"), lax.axis_index("gy")
    other = 1 - comp
    me = gx * N_GY + gy
    up, down = lax.rem(gx + N_GX - 1, N_GX), lax.rem(gx + 1, N_GX)
    left, right = lax.rem(gy + N_GY - 1, N_GY), lax.rem(gy + 1, N_GY)
    beside = ((comp, up, gy), (comp, down, gy), (comp, gx, left), (comp, gx, right))

    small = [
        pltpu.make_async_copy(source, target, sem_small.at[i])
        for i, (source, target) in enumerate(
            (
                (proj_hbm, proj),
                (land_hbm, land_row),
                (land_hbm, land_out),
                (table_hbm, table),
                (diff_hbm, diff),
                (recv_hbm, recv_out),
                (ip_hbm, ip),
            )
        )
    ]
    interior = pl.ds(TOP, ROWS)
    for copy in small[:3]:
        copy.start()
    get_state = pltpu.make_async_copy(state_hbm, ta.at[:, interior], sem_state)
    get_state.start()
    for copy in small[3:]:
        copy.start()
    get_vel = pltpu.make_async_copy(vel_hbm, vel, sem_vel)
    get_vel.start()

    barrier = pltpu.get_barrier_semaphore()
    for device in beside:
        pl.semaphore_signal(barrier, inc=1, device_id=device, device_id_type=MESH)

    def greet(d, carry):
        pl.semaphore_signal(
            barrier, inc=1, device_id=(other, lax.div(d, N_GY), lax.rem(d, N_GY)), device_id_type=MESH
        )
        return carry

    lax.fori_loop(0, GROUP, greet, 0)

    part = w_hbm.shape[0] // W_PARTS

    def get_w(i):
        rows = pl.ds(i * part, part)
        return pltpu.make_async_copy(w_hbm.at[rows], w_out.at[rows], sem_w.at[i])

    for i in range(W_PARTS):
        get_w(i).start()

    for copy in small:
        copy.wait()

    row_wet = jnp.where(comp == 0, jnp.ones((1, TILE), F32), land_row[...].astype(F32))
    wet[...] = jnp.transpose(jnp.broadcast_to(row_wet, (ROWS, TILE)))

    columns = [jnp.broadcast_to(proj[:, l : l + 1], (FLD, TILE)) for l in range(LEV)]
    get_state.wait()

    def export(i, carry):
        for j in range(4):
            x = i * 4 + j
            total = columns[0] * ta[0, pl.ds(TOP + x, 1), :]
            for l in range(1, LEV):
                total += columns[l] * ta[l, pl.ds(TOP + x, 1), :]
            ex[x] = total * jnp.where(comp == 0, 1.0, land_out[0, x].astype(F32))
        return carry

    lax.fori_loop(0, ROWS // 4, export, 0)
    pl.semaphore_wait(barrier, GROUP + 4)

    def serve(turn, carry):
        to_x, to_y = partner(turn, gx, gy)
        d = to_x * N_GY + to_y
        for q in range(CAP):
            buf[turn * CAP + q] = ex[table[comp, q, d]].astype(BF16)
        pltpu.make_async_remote_copy(
            src_ref=buf.at[pl.ds(turn * CAP, CAP)],
            dst_ref=arrived.at[pl.ds(me * CAP, CAP)],
            send_sem=sem_send,
            recv_sem=sem_recv,
            device_id=(other, to_x, to_y),
            device_id_type=MESH,
        ).start()
        return carry

    def pick(l):
        r = lax.broadcasted_iota(jnp.int32, (2 * LEV, TILE), 0)
        c = lax.broadcasted_iota(jnp.int32, (2 * LEV, TILE), 1)
        hit = ((r == l) & (c == 0)) | ((r == LEV + l) & (c == TILE - 1))
        return jnp.where(hit, 1.0, 0.0).astype(BF16)

    r = lax.broadcasted_iota(jnp.int32, (FLD, TILE), 0)
    c = lax.broadcasted_iota(jnp.int32, (FLD, TILE), 1)
    both_ends = jnp.where(((r == 0) & (c == 0)) | ((r == 1) & (c == TILE - 1)), 1.0, 0.0).astype(BF16)

    def halo_copy(turn, side):
        return pltpu.make_async_remote_copy(
            src_ref=halo_out.at[turn, side],
            dst_ref=halo_in.at[turn, side],
            send_sem=sem_hs.at[turn, side],
            recv_sem=sem_hr.at[turn, side],
            device_id=beside[side],
            device_id_type=MESH,
        )

    def send_halo(turn, t):
        flat = t.reshape(LEV * PADDED, TILE)
        halo_out[turn, 0] = flat[pl.ds(TOP, LEV, stride=PADDED), :].astype(BF16)
        halo_out[turn, 1] = flat[pl.ds(TOP + ROWS - 1, LEV, stride=PADDED), :].astype(BF16)

        for l in range(LEV):
            ends = lax.dot_general(
                both_ends, t[l, interior, :].astype(BF16), (((1,), (1,)), ((), ())), preferred_element_type=F32
            )
            edge[0, l : l + 1, :] = ends[0:1]
            edge[1, l : l + 1, :] = ends[1:2]
        halo_out[turn, 2] = edge[0].astype(BF16)
        halo_out[turn, 3] = edge[1].astype(BF16)
        for side in range(4):
            halo_copy(turn, side).start()

    def take_halo(turn, t):
        for side in range(4):
            halo_copy(turn, side).wait_recv()
        flat = t.reshape(LEV * PADDED, TILE)
        rows = [halo_in[turn, side].astype(F32) for side in range(4)]
        flat[pl.ds(TOP + ROWS, LEV, stride=PADDED), :] = jnp.where(gx < N_GX - 1, rows[0], 0.0)
        flat[pl.ds(TOP - 1, LEV, stride=PADDED), :] = jnp.where(gx > 0, rows[1], 0.0)
        last = jnp.where(gy < N_GY - 1, rows[2], 0.0)
        first = jnp.where(gy > 0, rows[3], 0.0)
        return jnp.transpose(jnp.concatenate([first, last], axis=0)).astype(BF16)

    def advance(t, edges, put):
        lane = lax.broadcasted_iota(jnp.int32, (ROWS, TILE), 1)

        def level(l, carry):
            mid = t[l, interior, :]
            above, below = t[l, pl.ds(TOP - 1, ROWS), :], t[l, pl.ds(TOP + 1, ROWS), :]
            sides = jnp.dot(edges, pick(l), preferred_element_type=F32)
            before = jnp.where(lane == 0, sides, pltpu.roll(mid, 1, 1))
            after = jnp.where(lane == TILE - 1, sides, pltpu.roll(mid, TILE - 1, 1))
            spread = above + below + before + after - 4.0 * mid
            carried = 0.5 * (
                vel[0, l].astype(F32) * (below - above) + vel[1, l].astype(F32) * (after - before)
            )
            put(l, mid + wet[...] * (diff[0, l] * spread - carried))
            return carry

        lax.fori_loop(0, LEV, level, 0)

    def put_tb(l, value):
        tb[l, interior, :] = value

    def put_tracer(l, value):
        tracer[l] = value

    lax.fori_loop(0, FIRST, serve, 0)
    send_halo(0, ta)
    lax.fori_loop(FIRST, SECOND, serve, 0)
    edges = take_halo(0, ta)
    get_vel.wait()
    advance(ta, edges, put_tb)
    send_halo(1, tb)
    lax.fori_loop(SECOND, GROUP, serve, 0)
    edges = take_halo(1, tb)
    advance(tb, edges, put_tracer)

    for f in range(FLD):
        for l in range(LEV):
            spread[f, l : l + 1, :] = jnp.full((1, TILE), ip[f, l], F32)
    for i in range(W_PARTS):
        get_w(i).wait()
    for turn in range(2):
        for side in range(4):
            halo_copy(turn, side).wait_send()
    pltpu.make_async_copy(buf, buf, sem_send).wait()
    pltpu.make_async_copy(arrived, arrived, sem_recv).wait()


def remap_kernel(chunk, recv, land, w, arrived, tracer, spread, new_hbm, imp_hbm, new, imp, sem_out):
    comp = lax.axis_index("comp")

    def out_copies(i):
        rows = pl.ds(pl.multiple_of(i * chunk, chunk), chunk)
        return (
            pltpu.make_async_copy(new.at[:, rows], new_hbm.at[:, rows], sem_out.at[0, i]),
            pltpu.make_async_copy(imp.at[rows], imp_hbm.at[rows], sem_out.at[1, i]),
        )

    tracer_rows = tracer.reshape(LEV * ROWS, TILE)
    new_rows = new.reshape(LEV * ROWS, TILE)

    def step(i, carry):
        for j in range(chunk):
            x = i * chunk + j
            wet = jnp.where(comp == 0, 1.0, land[0, x].astype(F32))
            source = jnp.concatenate([arrived[recv[k, x]] for k in range(K)], axis=1)
            weights = jnp.concatenate([w[x, k] for k in range(K)], axis=1)
            summed = lax.dot_general(source, weights, (((1,), (1,)), ((), ())), preferred_element_type=F32)
            got = (summed * wet).astype(BF16)
            imp[x] = got
            got = got.astype(F32)
            force = spread[0] * got[0:1, :]
            for f in range(1, FLD):
                force += spread[f] * got[f : f + 1, :]
            rows = pl.ds(x, LEV, stride=ROWS)
            new_rows[rows, :] = tracer_rows[rows, :] + wet * force
        for copy in out_copies(i):
            copy.start()
        return carry

    def drain(i, carry):
        for copy in out_copies(i):
            copy.wait()
        return carry

    lax.fori_loop(0, ROWS // chunk, step, 0)
    lax.fori_loop(0, ROWS // chunk, drain, 0)


ANY = pl.BlockSpec(memory_space=pl.ANY)
HBM = pl.BlockSpec(memory_space=pltpu.HBM)
VMEM = pl.BlockSpec(memory_space=pltpu.VMEM)
SMEM = pl.BlockSpec(memory_space=pltpu.SMEM)


def kept_in(space, arrays):
    return [pltpu.with_memory_space_constraint(a, space) for a in arrays]


def exchange(*arrays):
    dma = pltpu.SemaphoreType.DMA
    return pl.pallas_call(
        exchange_kernel,
        name="exchange",
        out_shape=(
            pltpu.VMEM((GROUP * CAP, FLD, TILE), BF16),
            pltpu.VMEM((LEV, ROWS, TILE), F32),
            pltpu.VMEM((ROWS, K, TILE, TILE), BF16),
            pltpu.VMEM((FLD, LEV, TILE), F32),
            pltpu.SMEM((K, ROWS), jnp.int32),
            pltpu.SMEM((1, ROWS), jnp.int32),
        ),
        in_specs=[HBM] * 9,
        out_specs=(VMEM, VMEM, VMEM, VMEM, SMEM, SMEM),
        scratch_shapes=[
            pltpu.VMEM((LEV, PADDED, TILE), F32),
            pltpu.VMEM((LEV, PADDED, TILE), F32),
            pltpu.VMEM((2, LEV, ROWS, TILE), BF16),
            pltpu.VMEM((ROWS, FLD, TILE), F32),
            pltpu.VMEM((GROUP * CAP, FLD, TILE), BF16),
            pltpu.VMEM((2, 4, LEV, TILE), BF16),
            pltpu.VMEM((2, 4, LEV, TILE), BF16),
            pltpu.VMEM((2, LEV, TILE), F32),
            pltpu.VMEM((ROWS, TILE), F32),
            pltpu.VMEM((FLD, LEV), F32),
            pltpu.VMEM((1, ROWS), jnp.int32),
            pltpu.SMEM((1, LEV), F32),
            pltpu.SMEM((2, CAP, GROUP), jnp.int32),
            pltpu.SMEM((FLD, LEV), F32),
            dma,
            dma,
            dma((7,)),
            dma((W_PARTS,)),
            dma,
            dma,
            dma((2, 4)),
            dma((2, 4)),
        ],
        compiler_params=pltpu.CompilerParams(collective_id=0, has_side_effects=True, vmem_limit_bytes=16 << 20),
    )(*kept_in(pltpu.HBM, arrays))


def remap(recv, land, weights, arrived, tracer, spread):
    chunk = 32
    return pl.pallas_call(
        functools.partial(remap_kernel, chunk),
        name="remap",
        out_shape=(
            jax.ShapeDtypeStruct((LEV, ROWS, TILE), F32),
            jax.ShapeDtypeStruct((ROWS, FLD, TILE), BF16),
        ),
        in_specs=[SMEM, SMEM, VMEM, VMEM, VMEM, VMEM],
        out_specs=(ANY, ANY),
        scratch_shapes=[
            pltpu.VMEM((LEV, ROWS, TILE), F32),
            pltpu.VMEM((ROWS, FLD, TILE), BF16),
            pltpu.SemaphoreType.DMA((2, ROWS // chunk)),
        ],
        compiler_params=pltpu.CompilerParams(vmem_limit_bytes=16 << 20),
    )(*kept_in(pltpu.SMEM, (recv, land)), *kept_in(pltpu.VMEM, (weights, arrived, tracer, spread)))


def per_device(
    state, velocity, diffusivity, export_proj, import_proj, intersection_weights, recv_slots, send_slots, land
):
    land = land.reshape(1, ROWS)
    table = send_slots[:, 0, 0].transpose(0, 2, 1)
    recv = recv_slots[0, :, 0].T
    arrived, tracer, weights, spread, recv, land = exchange(
        state[0], velocity[0], intersection_weights[0, :, 0], export_proj[0], diffusivity, table, land, recv,
        import_proj[0].T,
    )
    new_state, imported = remap(recv, land, weights, arrived, tracer, spread)
    return new_state[None], imported[None]


def solution(mesh):
    return jax.shard_map(
        per_device,
        mesh=mesh,
        in_specs=(
            P("comp", None, "gx", "gy"),
            P("comp", None, None, "gx", "gy"),
            P("comp", None),
            P("comp", None, None),
            P("comp", None, None),
            P("comp", "gx", "gy", None, None, None),
            P("comp", "gx", "gy", None),
            P(None, "gx", "gy", None, None),
            P("gx", "gy"),
        ),
        out_specs=(P("comp", None, "gx", "gy"), P("comp", "gx", None, "gy")),
        check_vma=False,
    )
```

```python
import functools

import jax
import jax.numpy as jnp
from jax import lax
from jax.experimental import pallas as pl
from jax.experimental.pallas import tpu as pltpu
from jax.sharding import PartitionSpec as P

MESH = pl.DeviceIdType.MESH
F32 = jnp.float32
BF16 = jnp.bfloat16

LEV, FLD, K = 16, 8, 4
ROWS, TILE = 128, 128
N_GX, N_GY = 8, 8
GROUP, CAP = 64, 16
TOP = 8
PADDED = ROWS + 2 * TOP
W_PARTS = 8
TURNED = 4
FIRST, SECOND = 16, 48


def partner(turn, gx, gy):
    block, i = lax.div(turn, 16), lax.rem(turn, 16)
    step_x = lax.rem(i, 4)
    step_y = lax.rem(lax.div(i, 4) + i, 4)
    step_high = lax.rem(i + block, 2)
    step_core = lax.div(block, 2)
    x = lax.rem(lax.div(gx, 2) + step_x, 4)
    core = lax.rem(gx + step_core, 2)
    y = lax.rem(lax.div(gy, 2) + step_y, 4)
    high = lax.rem(gy + step_high, 2)
    return x * 2 + core, y * 2 + high


def exchange_kernel(
    state_hbm, vel_hbm, w_hbm, proj_hbm, diff_hbm, table_hbm, land_hbm, recv_hbm, ip_hbm,
    arrived, tracer, w_out, spread, recv_out, land_out,
    ta, tb, vel, ex, buf, halo_out, halo_in, edge, wet, proj, land_row, diff, table, ip,
    sem_state, sem_vel, sem_small, sem_w, sem_send, sem_recv, sem_hs, sem_hr,
):
    comp, gx, gy = lax.axis_index("comp"), lax.axis_index("gx"), lax.axis_index("gy")
    other = 1 - comp
    me = gx * N_GY + gy
    up, down = lax.rem(gx + N_GX - 1, N_GX), lax.rem(gx + 1, N_GX)
    left, right = lax.rem(gy + N_GY - 1, N_GY), lax.rem(gy + 1, N_GY)
    beside = ((comp, up, gy), (comp, down, gy), (comp, gx, left), (comp, gx, right))

    small = [
        pltpu.make_async_copy(source, target, sem_small.at[i])
        for i, (source, target) in enumerate(
            (
                (proj_hbm, proj),
                (land_hbm, land_row),
                (land_hbm, land_out),
                (table_hbm, table),
                (diff_hbm, diff),
                (recv_hbm, recv_out),
                (ip_hbm, ip),
            )
        )
    ]
    interior = pl.ds(TOP, ROWS)
    for copy in small[:3]:
        copy.start()
    get_state = pltpu.make_async_copy(state_hbm, ta.at[:, interior], sem_state)
    get_state.start()
    for copy in small[3:]:
        copy.start()
    get_vel = pltpu.make_async_copy(vel_hbm, vel, sem_vel)
    get_vel.start()

    barrier = pltpu.get_barrier_semaphore()
    for device in beside:
        pl.semaphore_signal(barrier, inc=1, device_id=device, device_id_type=MESH)

    def greet(d, carry):
        pl.semaphore_signal(
            barrier, inc=1, device_id=(other, lax.div(d, N_GY), lax.rem(d, N_GY)), device_id_type=MESH
        )
        return carry

    lax.fori_loop(0, GROUP, greet, 0)

    part = w_hbm.shape[0] // W_PARTS

    def get_w(i):
        rows = pl.ds(i * part, part)
        return pltpu.make_async_copy(w_hbm.at[rows], w_out.at[rows], sem_w.at[i])

    for i in range(W_PARTS):
        get_w(i).start()

    for copy in small:
        copy.wait()

    row_wet = jnp.where(comp == 0, jnp.ones((1, TILE), F32), land_row[...].astype(F32))
    wet[...] = jnp.transpose(jnp.broadcast_to(row_wet, (ROWS, TILE)))

    columns = [jnp.broadcast_to(proj[:, l : l + 1], (FLD, TILE)) for l in range(LEV)]
    get_state.wait()

    def export(i, carry):
        for j in range(4):
            x = i * 4 + j
            total = columns[0] * ta[0, pl.ds(TOP + x, 1), :]
            for l in range(1, LEV):
                total += columns[l] * ta[l, pl.ds(TOP + x, 1), :]
            ex[x] = total * jnp.where(comp == 0, 1.0, land_out[0, x].astype(F32))
        return carry

    lax.fori_loop(0, ROWS // 4, export, 0)
    pl.semaphore_wait(barrier, GROUP + 4)

    def serve(turn, carry):
        to_x, to_y = partner(turn, gx, gy)
        d = to_x * N_GY + to_y
        for q in range(CAP):
            buf[turn * CAP + q] = ex[table[comp, q, d]].astype(BF16)
        pltpu.make_async_remote_copy(
            src_ref=buf.at[pl.ds(turn * CAP, CAP)],
            dst_ref=arrived.at[pl.ds(me * CAP, CAP)],
            send_sem=sem_send,
            recv_sem=sem_recv,
            device_id=(other, to_x, to_y),
            device_id_type=MESH,
        ).start()
        return carry

    def pick(l):
        r = lax.broadcasted_iota(jnp.int32, (2 * LEV, TILE), 0)
        c = lax.broadcasted_iota(jnp.int32, (2 * LEV, TILE), 1)
        hit = ((r == l) & (c == 0)) | ((r == LEV + l) & (c == TILE - 1))
        return jnp.where(hit, 1.0, 0.0).astype(BF16)

    r = lax.broadcasted_iota(jnp.int32, (FLD, TILE), 0)
    c = lax.broadcasted_iota(jnp.int32, (FLD, TILE), 1)
    both_ends = jnp.where(((r == 0) & (c == 0)) | ((r == 1) & (c == TILE - 1)), 1.0, 0.0).astype(BF16)

    def halo_copy(turn, side):
        return pltpu.make_async_remote_copy(
            src_ref=halo_out.at[turn, side],
            dst_ref=halo_in.at[turn, side],
            send_sem=sem_hs.at[turn, side],
            recv_sem=sem_hr.at[turn, side],
            device_id=beside[side],
            device_id_type=MESH,
        )

    def send_halo(turn, t):
        flat = t.reshape(LEV * PADDED, TILE)
        halo_out[turn, 0] = flat[pl.ds(TOP, LEV, stride=PADDED), :].astype(BF16)
        halo_out[turn, 1] = flat[pl.ds(TOP + ROWS - 1, LEV, stride=PADDED), :].astype(BF16)

        for l in range(LEV):
            ends = lax.dot_general(
                both_ends, t[l, interior, :].astype(BF16), (((1,), (1,)), ((), ())), preferred_element_type=F32
            )
            edge[0, l : l + 1, :] = ends[0:1]
            edge[1, l : l + 1, :] = ends[1:2]
        halo_out[turn, 2] = edge[0].astype(BF16)
        halo_out[turn, 3] = edge[1].astype(BF16)
        for side in range(4):
            halo_copy(turn, side).start()

    def take_halo(turn, t):
        for side in range(4):
            halo_copy(turn, side).wait_recv()
        flat = t.reshape(LEV * PADDED, TILE)
        rows = [halo_in[turn, side].astype(F32) for side in range(4)]
        flat[pl.ds(TOP + ROWS, LEV, stride=PADDED), :] = jnp.where(gx < N_GX - 1, rows[0], 0.0)
        flat[pl.ds(TOP - 1, LEV, stride=PADDED), :] = jnp.where(gx > 0, rows[1], 0.0)
        last = jnp.where(gy < N_GY - 1, rows[2], 0.0)
        first = jnp.where(gy > 0, rows[3], 0.0)
        return jnp.transpose(jnp.concatenate([first, last], axis=0)).astype(BF16)

    def advance(t, edges, put):
        lane = lax.broadcasted_iota(jnp.int32, (ROWS, TILE), 1)

        def level(l, carry):
            mid = t[l, interior, :]
            above, below = t[l, pl.ds(TOP - 1, ROWS), :], t[l, pl.ds(TOP + 1, ROWS), :]
            sides = jnp.dot(edges, pick(l), preferred_element_type=F32)
            before = jnp.where(lane == 0, sides, pltpu.roll(mid, 1, 1))
            after = jnp.where(lane == TILE - 1, sides, pltpu.roll(mid, TILE - 1, 1))
            spread = above + below + before + after - 4.0 * mid
            carried = 0.5 * (
                vel[0, l].astype(F32) * (below - above) + vel[1, l].astype(F32) * (after - before)
            )
            put(l, mid + wet[...] * (diff[0, l] * spread - carried))
            return carry

        lax.fori_loop(0, LEV, level, 0)

    def put_tb(l, value):
        tb[l, interior, :] = value

    def put_tracer(l, value):
        tracer[l] = value

    lax.fori_loop(0, FIRST, serve, 0)
    send_halo(0, ta)
    lax.fori_loop(FIRST, SECOND, serve, 0)
    edges = take_halo(0, ta)
    get_vel.wait()
    advance(ta, edges, put_tb)
    send_halo(1, tb)
    lax.fori_loop(SECOND, GROUP, serve, 0)

    def turn_w(i, carry):
        for j in range(TURNED):
            for k in range(K):
                w_out[i * TURNED + j, k] = jnp.transpose(w_out[i * TURNED + j, k])
        return carry

    for i in range(W_PARTS):
        get_w(i).wait()
    lax.fori_loop(0, ROWS // TURNED, turn_w, 0)
    edges = take_halo(1, tb)
    advance(tb, edges, put_tracer)

    for f in range(FLD):
        for l in range(LEV):
            spread[f, l : l + 1, :] = jnp.full((1, TILE), ip[f, l], F32)
    for turn in range(2):
        for side in range(4):
            halo_copy(turn, side).wait_send()
    pltpu.make_async_copy(buf, buf, sem_send).wait()
    pltpu.make_async_copy(arrived, arrived, sem_recv).wait()


def remap_kernel(chunk, recv, land, w, arrived, tracer, spread, new_hbm, imp_hbm, new, imp, sem_out):
    comp = lax.axis_index("comp")

    def out_copies(i):
        rows = pl.ds(pl.multiple_of(i * chunk, chunk), chunk)
        return (
            pltpu.make_async_copy(new.at[:, rows], new_hbm.at[:, rows], sem_out.at[0, i]),
            pltpu.make_async_copy(imp.at[rows], imp_hbm.at[rows], sem_out.at[1, i]),
        )

    tracer_rows = tracer.reshape(LEV * ROWS, TILE)
    new_rows = new.reshape(LEV * ROWS, TILE)

    def step(i, carry):
        for j in range(chunk):
            x = i * chunk + j
            wet = jnp.where(comp == 0, 1.0, land[0, x].astype(F32))
            source = jnp.concatenate([arrived[recv[k, x]] for k in range(K)], axis=1)
            weights = jnp.concatenate([w[x, k] for k in range(K)], axis=0)
            summed = jnp.dot(source, weights, preferred_element_type=F32)
            got = (summed * wet).astype(BF16)
            imp[x] = got
            got = got.astype(F32)
            force = spread[0] * got[0:1, :]
            for f in range(1, FLD):
                force += spread[f] * got[f : f + 1, :]
            rows = pl.ds(x, LEV, stride=ROWS)
            new_rows[rows, :] = tracer_rows[rows, :] + wet * force
        for copy in out_copies(i):
            copy.start()
        return carry

    def drain(i, carry):
        for copy in out_copies(i):
            copy.wait()
        return carry

    lax.fori_loop(0, ROWS // chunk, step, 0)
    lax.fori_loop(0, ROWS // chunk, drain, 0)


ANY = pl.BlockSpec(memory_space=pl.ANY)
HBM = pl.BlockSpec(memory_space=pltpu.HBM)
VMEM = pl.BlockSpec(memory_space=pltpu.VMEM)
SMEM = pl.BlockSpec(memory_space=pltpu.SMEM)


def kept_in(space, arrays):
    return [pltpu.with_memory_space_constraint(a, space) for a in arrays]


def exchange(*arrays):
    dma = pltpu.SemaphoreType.DMA
    return pl.pallas_call(
        exchange_kernel,
        name="exchange",
        out_shape=(
            pltpu.VMEM((GROUP * CAP, FLD, TILE), BF16),
            pltpu.VMEM((LEV, ROWS, TILE), F32),
            pltpu.VMEM((ROWS, K, TILE, TILE), BF16),
            pltpu.VMEM((FLD, LEV, TILE), F32),
            pltpu.SMEM((K, ROWS), jnp.int32),
            pltpu.SMEM((1, ROWS), jnp.int32),
        ),
        in_specs=[HBM] * 9,
        out_specs=(VMEM, VMEM, VMEM, VMEM, SMEM, SMEM),
        scratch_shapes=[
            pltpu.VMEM((LEV, PADDED, TILE), F32),
            pltpu.VMEM((LEV, PADDED, TILE), F32),
            pltpu.VMEM((2, LEV, ROWS, TILE), BF16),
            pltpu.VMEM((ROWS, FLD, TILE), F32),
            pltpu.VMEM((GROUP * CAP, FLD, TILE), BF16),
            pltpu.VMEM((2, 4, LEV, TILE), BF16),
            pltpu.VMEM((2, 4, LEV, TILE), BF16),
            pltpu.VMEM((2, LEV, TILE), F32),
            pltpu.VMEM((ROWS, TILE), F32),
            pltpu.VMEM((FLD, LEV), F32),
            pltpu.VMEM((1, ROWS), jnp.int32),
            pltpu.SMEM((1, LEV), F32),
            pltpu.SMEM((2, CAP, GROUP), jnp.int32),
            pltpu.SMEM((FLD, LEV), F32),
            dma,
            dma,
            dma((7,)),
            dma((W_PARTS,)),
            dma,
            dma,
            dma((2, 4)),
            dma((2, 4)),
        ],
        compiler_params=pltpu.CompilerParams(collective_id=0, has_side_effects=True, vmem_limit_bytes=16 << 20),
    )(*kept_in(pltpu.HBM, arrays))


def remap(recv, land, weights, arrived, tracer, spread):
    chunk = 32
    return pl.pallas_call(
        functools.partial(remap_kernel, chunk),
        name="remap",
        out_shape=(
            jax.ShapeDtypeStruct((LEV, ROWS, TILE), F32),
            jax.ShapeDtypeStruct((ROWS, FLD, TILE), BF16),
        ),
        in_specs=[SMEM, SMEM, VMEM, VMEM, VMEM, VMEM],
        out_specs=(ANY, ANY),
        scratch_shapes=[
            pltpu.VMEM((LEV, ROWS, TILE), F32),
            pltpu.VMEM((ROWS, FLD, TILE), BF16),
            pltpu.SemaphoreType.DMA((2, ROWS // chunk)),
        ],
        compiler_params=pltpu.CompilerParams(vmem_limit_bytes=16 << 20),
    )(*kept_in(pltpu.SMEM, (recv, land)), *kept_in(pltpu.VMEM, (weights, arrived, tracer, spread)))


def per_device(
    state, velocity, diffusivity, export_proj, import_proj, intersection_weights, recv_slots, send_slots, land
):
    land = land.reshape(1, ROWS)
    table = send_slots[:, 0, 0].transpose(0, 2, 1)
    recv = recv_slots[0, :, 0].T
    arrived, tracer, weights, spread, recv, land = exchange(
        state[0], velocity[0], intersection_weights[0, :, 0], export_proj[0], diffusivity, table, land, recv,
        import_proj[0].T,
    )
    new_state, imported = remap(recv, land, weights, arrived, tracer, spread)
    return new_state[None], imported[None]


def solution(mesh):
    return jax.shard_map(
        per_device,
        mesh=mesh,
        in_specs=(
            P("comp", None, "gx", "gy"),
            P("comp", None, None, "gx", "gy"),
            P("comp", None),
            P("comp", None, None),
            P("comp", None, None),
            P("comp", "gx", "gy", None, None, None),
            P("comp", "gx", "gy", None),
            P(None, "gx", "gy", None, None),
            P("gx", "gy"),
        ),
        out_specs=(P("comp", None, "gx", "gy"), P("comp", "gx", None, "gy")),
        check_vma=False,
    )
```

```python
import jax
import jax.numpy as jnp
from jax import lax
from jax.experimental import pallas as pl
from jax.experimental.pallas import tpu as pltpu
from jax.sharding import PartitionSpec as P

MESH = pl.DeviceIdType.MESH
F32 = jnp.float32
BF16 = jnp.bfloat16

LEV, FLD, K = 16, 8, 4
ROWS, TILE = 128, 128
N_GX, N_GY = 8, 8
GROUP, CAP = 64, 16
TOP = 8
PADDED = ROWS + 2 * TOP
W_PARTS = 8
S_PARTS = 4
OUT_ROWS = 8
TURNED = 4
FIRST, SECOND = 4, 36


def partner(turn, gx, gy):
    block, i = lax.div(turn, 16), lax.rem(turn, 16)
    step_x = lax.rem(i, 4)
    step_y = lax.rem(lax.div(i, 4) + i, 4)
    step_high = lax.rem(i + block, 2)
    step_core = lax.div(block, 2)
    x = lax.rem(lax.div(gx, 2) + step_x, 4)
    core = lax.rem(gx + step_core, 2)
    y = lax.rem(lax.div(gy, 2) + step_y, 4)
    high = lax.rem(gy + step_high, 2)
    return x * 2 + core, y * 2 + high


def exchange_kernel(
    state_hbm, vel_hbm, w_hbm, proj_hbm, diff_hbm, table_hbm, land_hbm, recv_hbm, ip_hbm,
    arrived, tracer, w_out, spread, recv_out, land_out,
    ta, tb, vel, ex, buf, halo_out, halo_in, edge, wet, proj, land_row, diff, table, ip,
    sem_state, sem_vel, sem_small, sem_w, sem_send, sem_recv, sem_hs, sem_hr,
):
    comp, gx, gy = lax.axis_index("comp"), lax.axis_index("gx"), lax.axis_index("gy")
    other = 1 - comp
    me = gx * N_GY + gy
    up, down = lax.rem(gx + N_GX - 1, N_GX), lax.rem(gx + 1, N_GX)
    left, right = lax.rem(gy + N_GY - 1, N_GY), lax.rem(gy + 1, N_GY)
    beside = ((comp, up, gy), (comp, down, gy), (comp, gx, left), (comp, gx, right))

    small = [
        pltpu.make_async_copy(source, target, sem_small.at[i])
        for i, (source, target) in enumerate(
            (
                (proj_hbm, proj),
                (land_hbm, land_out),
                (table_hbm, table),
                (land_hbm, land_row),
                (diff_hbm, diff),
                (recv_hbm, recv_out),
                (ip_hbm, ip),
            )
        )
    ]
    interior = pl.ds(TOP, ROWS)
    slab = ROWS // S_PARTS

    def get_state(i):
        return pltpu.make_async_copy(
            state_hbm.at[:, pl.ds(i * slab, slab)], ta.at[:, pl.ds(TOP + i * slab, slab)], sem_state.at[i]
        )

    for i in range(S_PARTS):
        get_state(i).start()
    barrier = pltpu.get_barrier_semaphore()
    for d in range(GROUP):
        pl.semaphore_signal(barrier, inc=1, device_id=(other, d // N_GY, d % N_GY), device_id_type=MESH)
    for device in beside:
        pl.semaphore_signal(barrier, inc=1, device_id=device, device_id_type=MESH)
    for copy in small:
        copy.start()
    get_vel = pltpu.make_async_copy(vel_hbm, vel, sem_vel)
    get_vel.start()

    part = w_hbm.shape[0] // W_PARTS

    def get_w(i):
        rows = pl.ds(i * part, part)
        return pltpu.make_async_copy(w_hbm.at[rows], w_out.at[rows], sem_w.at[i])

    for i in range(W_PARTS):
        get_w(i).start()

    for copy in small[:3]:
        copy.wait()
    columns = [jnp.broadcast_to(proj[:, l : l + 1], (FLD, TILE)) for l in range(LEV)]

    def export(i, carry):
        for j in range(8):
            x = i * 8 + j
            total = columns[0] * ta[0, pl.ds(TOP + x, 1), :]
            for l in range(1, LEV):
                total += columns[l] * ta[l, pl.ds(TOP + x, 1), :]
            ex[x] = total * jnp.where(comp == 0, 1.0, land_out[0, x].astype(F32))
        return carry

    for i in range(S_PARTS):
        get_state(i).wait()
        lax.fori_loop(i * slab // 8, (i + 1) * slab // 8, export, 0)
    pl.semaphore_wait(barrier, GROUP + 4)

    def serve(turn, carry):
        to_x, to_y = partner(turn, gx, gy)
        d = to_x * N_GY + to_y
        for q in range(CAP):
            buf[turn * CAP + q] = ex[table[comp, q, d]].astype(BF16)
        pltpu.make_async_remote_copy(
            src_ref=buf.at[pl.ds(turn * CAP, CAP)],
            dst_ref=arrived.at[pl.ds(me * CAP, CAP)],
            send_sem=sem_send,
            recv_sem=sem_recv,
            device_id=(other, to_x, to_y),
            device_id_type=MESH,
        ).start()
        return carry

    def pick(l):
        r = lax.broadcasted_iota(jnp.int32, (2 * LEV, TILE), 0)
        c = lax.broadcasted_iota(jnp.int32, (2 * LEV, TILE), 1)
        hit = ((r == l) & (c == 0)) | ((r == LEV + l) & (c == TILE - 1))
        return jnp.where(hit, 1.0, 0.0).astype(BF16)

    r = lax.broadcasted_iota(jnp.int32, (FLD, TILE), 0)
    c = lax.broadcasted_iota(jnp.int32, (FLD, TILE), 1)
    both_ends = jnp.where(((r == 0) & (c == 0)) | ((r == 1) & (c == TILE - 1)), 1.0, 0.0).astype(BF16)

    def halo_copy(turn, side):
        return pltpu.make_async_remote_copy(
            src_ref=halo_out.at[turn, side],
            dst_ref=halo_in.at[turn, side],
            send_sem=sem_hs.at[turn, side],
            recv_sem=sem_hr.at[turn, side],
            device_id=beside[side],
            device_id_type=MESH,
        )

    def send_halo(turn, t):
        flat = t.reshape(LEV * PADDED, TILE)
        halo_out[turn, 0] = flat[pl.ds(TOP, LEV, stride=PADDED), :].astype(BF16)
        halo_out[turn, 1] = flat[pl.ds(TOP + ROWS - 1, LEV, stride=PADDED), :].astype(BF16)

        for l in range(LEV):
            ends = lax.dot_general(
                both_ends, t[l, interior, :].astype(BF16), (((1,), (1,)), ((), ())), preferred_element_type=F32
            )
            edge[0, l : l + 1, :] = ends[0:1]
            edge[1, l : l + 1, :] = ends[1:2]
        halo_out[turn, 2] = edge[0].astype(BF16)
        halo_out[turn, 3] = edge[1].astype(BF16)
        for side in range(4):
            halo_copy(turn, side).start()

    def take_halo(turn, t):
        for side in range(4):
            halo_copy(turn, side).wait_recv()
        flat = t.reshape(LEV * PADDED, TILE)
        rows = [halo_in[turn, side].astype(F32) for side in range(4)]
        flat[pl.ds(TOP + ROWS, LEV, stride=PADDED), :] = jnp.where(gx < N_GX - 1, rows[0], 0.0)
        flat[pl.ds(TOP - 1, LEV, stride=PADDED), :] = jnp.where(gx > 0, rows[1], 0.0)
        last = jnp.where(gy < N_GY - 1, rows[2], 0.0)
        first = jnp.where(gy > 0, rows[3], 0.0)
        return jnp.transpose(jnp.concatenate([first, last], axis=0)).astype(BF16)

    def advance(t, edges, put):
        lane = lax.broadcasted_iota(jnp.int32, (ROWS, TILE), 1)

        def level(l, carry):
            mid = t[l, interior, :]
            above, below = t[l, pl.ds(TOP - 1, ROWS), :], t[l, pl.ds(TOP + 1, ROWS), :]
            sides = jnp.dot(edges, pick(l), preferred_element_type=F32)
            before = jnp.where(lane == 0, sides, pltpu.roll(mid, 1, 1))
            after = jnp.where(lane == TILE - 1, sides, pltpu.roll(mid, TILE - 1, 1))
            spread = above + below + before + after - 4.0 * mid
            carried = 0.5 * (
                vel[0, l].astype(F32) * (below - above) + vel[1, l].astype(F32) * (after - before)
            )
            put(l, mid + wet[...] * (diff[0, l] * spread - carried))
            return carry

        lax.fori_loop(0, LEV, level, 0)

    def put_tb(l, value):
        tb[l, interior, :] = value

    def put_tracer(l, value):
        tracer[l] = value

    lax.fori_loop(0, FIRST, serve, 0)
    for copy in small[3:]:
        copy.wait()
    row_wet = jnp.where(comp == 0, jnp.ones((1, TILE), F32), land_row[...].astype(F32))
    wet[...] = jnp.transpose(jnp.broadcast_to(row_wet, (ROWS, TILE)))
    send_halo(0, ta)
    lax.fori_loop(FIRST, SECOND, serve, 0)
    edges = take_halo(0, ta)
    get_vel.wait()
    advance(ta, edges, put_tb)
    send_halo(1, tb)
    lax.fori_loop(SECOND, GROUP, serve, 0)

    def turn_w(i, carry):
        for j in range(TURNED):
            for k in range(K):
                w_out[i * TURNED + j, k] = jnp.transpose(w_out[i * TURNED + j, k])
        return carry

    for i in range(W_PARTS):
        get_w(i).wait()
    lax.fori_loop(0, ROWS // TURNED, turn_w, 0)
    edges = take_halo(1, tb)
    advance(tb, edges, put_tracer)

    for f in range(FLD):
        for l in range(LEV):
            spread[f, l : l + 1, :] = jnp.full((1, TILE), ip[f, l], F32)
    for turn in range(2):
        for side in range(4):
            halo_copy(turn, side).wait_send()
    pltpu.make_async_copy(buf, buf, sem_send).wait()
    pltpu.make_async_copy(arrived, arrived, sem_recv).wait()


def remap_kernel(recv, land, w, arrived, tracer, spread, new_hbm, imp_hbm, new, imp, sem_out):
    comp = lax.axis_index("comp")
    tracer_rows = tracer.reshape(LEV * ROWS, TILE)
    new_rows = new.reshape(LEV * ROWS, TILE)
    copies = []
    for x in range(ROWS):
        wet = jnp.where(comp == 0, 1.0, land[0, x].astype(F32))
        source = jnp.concatenate([arrived[recv[k, x]] for k in range(K)], axis=1)
        weights = jnp.concatenate([w[x, k] for k in range(K)], axis=0)
        got = (jnp.dot(source, weights, preferred_element_type=F32) * wet).astype(BF16)
        imp[x] = got
        got = got.astype(F32)
        force = spread[0] * got[0:1, :]
        for f in range(1, FLD):
            force += spread[f] * got[f : f + 1, :]
        rows = pl.ds(x, LEV, stride=ROWS)
        new_rows[rows, :] = tracer_rows[rows, :] + wet * force
        if x % OUT_ROWS == OUT_ROWS - 1:
            i = x // OUT_ROWS
            done = pl.ds(i * OUT_ROWS, OUT_ROWS)
            copies.append(pltpu.make_async_copy(new.at[:, done], new_hbm.at[:, done], sem_out.at[0, i]))
            copies.append(pltpu.make_async_copy(imp.at[done], imp_hbm.at[done], sem_out.at[1, i]))
            copies[-2].start()
            copies[-1].start()
    for copy in copies:
        copy.wait()


ANY = pl.BlockSpec(memory_space=pl.ANY)
HBM = pl.BlockSpec(memory_space=pltpu.HBM)
VMEM = pl.BlockSpec(memory_space=pltpu.VMEM)
SMEM = pl.BlockSpec(memory_space=pltpu.SMEM)


def kept_in(space, arrays):
    return [pltpu.with_memory_space_constraint(a, space) for a in arrays]


def exchange(*arrays):
    dma = pltpu.SemaphoreType.DMA
    return pl.pallas_call(
        exchange_kernel,
        name="exchange",
        out_shape=(
            pltpu.VMEM((GROUP * CAP, FLD, TILE), BF16),
            pltpu.VMEM((LEV, ROWS, TILE), F32),
            pltpu.VMEM((ROWS, K, TILE, TILE), BF16),
            pltpu.VMEM((FLD, LEV, TILE), F32),
            pltpu.SMEM((K, ROWS), jnp.int32),
            pltpu.SMEM((1, ROWS), jnp.int32),
        ),
        in_specs=[HBM] * 9,
        out_specs=(VMEM, VMEM, VMEM, VMEM, SMEM, SMEM),
        scratch_shapes=[
            pltpu.VMEM((LEV, PADDED, TILE), F32),
            pltpu.VMEM((LEV, PADDED, TILE), F32),
            pltpu.VMEM((2, LEV, ROWS, TILE), BF16),
            pltpu.VMEM((ROWS, FLD, TILE), F32),
            pltpu.VMEM((GROUP * CAP, FLD, TILE), BF16),
            pltpu.VMEM((2, 4, LEV, TILE), BF16),
            pltpu.VMEM((2, 4, LEV, TILE), BF16),
            pltpu.VMEM((2, LEV, TILE), F32),
            pltpu.VMEM((ROWS, TILE), F32),
            pltpu.VMEM((FLD, LEV), F32),
            pltpu.VMEM((1, ROWS), jnp.int32),
            pltpu.SMEM((1, LEV), F32),
            pltpu.SMEM((2, CAP, GROUP), jnp.int32),
            pltpu.SMEM((FLD, LEV), F32),
            dma((S_PARTS,)),
            dma,
            dma((7,)),
            dma((W_PARTS,)),
            dma,
            dma,
            dma((2, 4)),
            dma((2, 4)),
        ],
        compiler_params=pltpu.CompilerParams(collective_id=0, has_side_effects=True, vmem_limit_bytes=16 << 20),
    )(*kept_in(pltpu.HBM, arrays))


def remap(recv, land, weights, arrived, tracer, spread):
    return pl.pallas_call(
        remap_kernel,
        name="remap",
        out_shape=(
            jax.ShapeDtypeStruct((LEV, ROWS, TILE), F32),
            jax.ShapeDtypeStruct((ROWS, FLD, TILE), BF16),
        ),
        in_specs=[SMEM, SMEM, VMEM, VMEM, VMEM, VMEM],
        out_specs=(ANY, ANY),
        scratch_shapes=[
            pltpu.VMEM((LEV, ROWS, TILE), F32),
            pltpu.VMEM((ROWS, FLD, TILE), BF16),
            pltpu.SemaphoreType.DMA((2, ROWS // OUT_ROWS)),
        ],
        compiler_params=pltpu.CompilerParams(vmem_limit_bytes=16 << 20),
    )(*kept_in(pltpu.SMEM, (recv, land)), *kept_in(pltpu.VMEM, (weights, arrived, tracer, spread)))


def per_device(
    state, velocity, diffusivity, export_proj, import_proj, intersection_weights, recv_slots, send_slots, land
):
    land = land.reshape(1, ROWS)
    table = send_slots[:, 0, 0].transpose(0, 2, 1)
    recv = recv_slots[0, :, 0].T
    arrived, tracer, weights, spread, recv, land = exchange(
        state[0], velocity[0], intersection_weights[0, :, 0], export_proj[0], diffusivity, table, land, recv,
        import_proj[0].T,
    )
    new_state, imported = remap(recv, land, weights, arrived, tracer, spread)
    return new_state[None], imported[None]


def solution(mesh):
    return jax.shard_map(
        per_device,
        mesh=mesh,
        in_specs=(
            P("comp", None, "gx", "gy"),
            P("comp", None, None, "gx", "gy"),
            P("comp", None),
            P("comp", None, None),
            P("comp", None, None),
            P("comp", "gx", "gy", None, None, None),
            P("comp", "gx", "gy", None),
            P(None, "gx", "gy", None, None),
            P("gx", "gy"),
        ),
        out_specs=(P("comp", None, "gx", "gy"), P("comp", "gx", None, "gy")),
        check_vma=False,
    )
```

```python
import jax
import jax.numpy as jnp
from jax import lax
from jax.experimental import pallas as pl
from jax.experimental.pallas import tpu as pltpu
from jax.sharding import PartitionSpec as P

MESH = pl.DeviceIdType.MESH
F32 = jnp.float32
BF16 = jnp.bfloat16

LEV, FLD, K = 16, 8, 4
ROWS, TILE = 128, 128
N_GX, N_GY = 8, 8
GROUP, CAP = 64, 16
TOP = 8
PADDED = ROWS + 2 * TOP
W_PARTS = 8
S_PARTS = 4
OUT_ROWS = 8
TURNED = 4
SELF = 2 * CAP
EACH = tuple((core, high) for core in range(2) for high in range(2))
STRAIGHT = ((1, 1), (3, 3))
VIA_Z = ((0, 1), (1, 0), (0, 3), (3, 0), (1, 3), (3, 1), (0, 0))
NEAR = (0, 1, 3)


def place(gx, gy, dx, core, dy, high):
    to_x = lax.rem(lax.div(gx, 2) + dx, 4) * 2 + lax.rem(gx + core, 2)
    to_y = lax.rem(lax.div(gy, 2) + dy, 4) * 2 + lax.rem(gy + high, 2)
    return to_x, to_y


def exchange_kernel(
    state_hbm, vel_hbm, w_hbm, proj_hbm, diff_hbm, table_hbm, land_hbm, recv_hbm, ip_hbm,
    arrived, tracer, w_out, spread, recv_out, land_out,
    ta, tb, vel, ex, near, across, far_x, far_y, tab_in, buf,
    halo_out, halo_in, edge, wet, proj, land_row, diff, table, tabs, ip,
    sem_state, sem_vel, sem_small, sem_w, sem_send, sem_recv, sem_hs, sem_hr,
    sem_gs, sem_gr, sem_ts, sem_tr, sem_tabs,
):
    comp, gx, gy = lax.axis_index("comp"), lax.axis_index("gx"), lax.axis_index("gy")
    other = 1 - comp
    me = gx * N_GY + gy
    up, down = lax.rem(gx + N_GX - 1, N_GX), lax.rem(gx + 1, N_GX)
    left, right = lax.rem(gy + N_GY - 1, N_GY), lax.rem(gy + 1, N_GY)
    beside = ((comp, up, gy), (comp, down, gy), (comp, gx, left), (comp, gx, right))

    small = [
        pltpu.make_async_copy(source, target, sem_small.at[i])
        for i, (source, target) in enumerate(
            (
                (proj_hbm, proj),
                (land_hbm, land_out),
                (table_hbm, table),
                (land_hbm, land_row),
                (diff_hbm, diff),
                (recv_hbm, recv_out),
                (ip_hbm, ip),
            )
        )
    ]
    interior = pl.ds(TOP, ROWS)
    slab = ROWS // S_PARTS

    def get_state(i):
        return pltpu.make_async_copy(
            state_hbm.at[:, pl.ds(i * slab, slab)], ta.at[:, pl.ds(TOP + i * slab, slab)], sem_state.at[i]
        )

    for i in range(S_PARTS):
        get_state(i).start()
    barrier = pltpu.get_barrier_semaphore()
    peers = [(other, *place(gx, gy, dx, core, dy, high)) for dx, dy in STRAIGHT for core, high in EACH]
    peers += [(other, *place(gx, gy, 0, core, dy, high)) for dy in range(4) for core, high in EACH]
    peers += [(other, *place(gx, gy, dx, core, 0, high)) for dx in range(1, 4) for core, high in EACH]
    peers += [(comp, *place(gx, gy, dx, core, dy, 0)) for dx, dy in VIA_Z for core in range(2) if dx or dy or core]
    peers += [(comp, *place(gx, gy, 2, 0, 0, 0)), (comp, *place(gx, gy, 0, 0, 2, 0)), *beside]
    for device in peers:
        pl.semaphore_signal(barrier, inc=1, device_id=device, device_id_type=MESH)
    for copy in small:
        copy.start()
    get_vel = pltpu.make_async_copy(vel_hbm, vel, sem_vel)
    get_vel.start()

    part = w_hbm.shape[0] // W_PARTS

    def get_w(i):
        rows = pl.ds(i * part, part)
        return pltpu.make_async_copy(w_hbm.at[rows], w_out.at[rows], sem_w.at[i])

    for i in range(W_PARTS):
        get_w(i).start()

    for copy in small[:3]:
        copy.wait()
    columns = [jnp.broadcast_to(proj[:, l : l + 1], (FLD, TILE)) for l in range(LEV)]

    def export(i, carry):
        for j in range(8):
            x = i * 8 + j
            total = columns[0] * ta[0, pl.ds(TOP + x, 1), :]
            for l in range(1, LEV):
                total += columns[l] * ta[l, pl.ds(TOP + x, 1), :]
            ex[x] = (total * jnp.where(comp == 0, 1.0, land_out[0, x].astype(F32))).astype(BF16)
        return carry

    for i in range(S_PARTS):
        get_state(i).wait()
        lax.fori_loop(i * slab // 8, (i + 1) * slab // 8, export, 0)
    r = lax.broadcasted_iota(jnp.int32, (FLD, TILE), 0)
    c = lax.broadcasted_iota(jnp.int32, (FLD, TILE), 1)
    both_ends = jnp.where(((r == 0) & (c == 0)) | ((r == 1) & (c == TILE - 1)), 1.0, 0.0).astype(BF16)

    def halo_copy(turn, side):
        return pltpu.make_async_remote_copy(
            src_ref=halo_out.at[turn, side],
            dst_ref=halo_in.at[turn, side],
            send_sem=sem_hs.at[turn, side],
            recv_sem=sem_hr.at[turn, side],
            device_id=beside[side],
            device_id_type=MESH,
        )

    def make_halo(turn, t):
        flat = t.reshape(LEV * PADDED, TILE)
        halo_out[turn, 0] = flat[pl.ds(TOP, LEV, stride=PADDED), :].astype(BF16)
        halo_out[turn, 1] = flat[pl.ds(TOP + ROWS - 1, LEV, stride=PADDED), :].astype(BF16)

        for l in range(LEV):
            ends = lax.dot_general(
                both_ends, t[l, interior, :].astype(BF16), (((1,), (1,)), ((), ())), preferred_element_type=F32
            )
            edge[0, l : l + 1, :] = ends[0:1]
            edge[1, l : l + 1, :] = ends[1:2]
        halo_out[turn, 2] = edge[0].astype(BF16)
        halo_out[turn, 3] = edge[1].astype(BF16)

    make_halo(0, ta)
    pl.semaphore_wait(barrier, len(peers))

    far = lambda g: lax.rem(g + 4, 8)
    gy_pair = lax.div(gy, 2) * 2
    gy_twin = gy_pair + 1 - lax.rem(gy, 2)
    relays = ((other, gx, gy), (other, gx, gy_twin), (comp, far(gx), gy), (comp, gx, far(gy)))
    taken = (near, across, far_x, far_y)

    def gather(i):
        return pltpu.make_async_remote_copy(
            src_ref=ex, dst_ref=taken[i], send_sem=sem_gs.at[i], recv_sem=sem_gr.at[i],
            device_id=relays[i], device_id_type=MESH,
        )

    def gather_table(i):
        return pltpu.make_async_remote_copy(
            src_ref=table_hbm.at[comp], dst_ref=tab_in.at[i - 1], send_sem=sem_ts.at[i - 1], recv_sem=sem_tr.at[i - 1],
            device_id=relays[i], device_id_type=MESH,
        )

    def fill(base, tiles, places, d):
        for q in range(CAP):
            buf[base + q] = tiles[places(q, d)]

    def send(base, count, source, device):
        pltpu.make_async_remote_copy(
            src_ref=buf.at[pl.ds(base, count)],
            dst_ref=arrived.at[pl.ds(source * CAP, count)],
            send_sem=sem_send,
            recv_sem=sem_recv,
            device_id=device,
            device_id_type=MESH,
        ).start()

    own_places = lambda q, d: table[comp, q, d]
    near_places = lambda q, d: table[other, q, d]
    across_places = lambda q, d: tabs[0, q, d]
    far_x_places = lambda q, d: tabs[1, q, d]
    far_y_places = lambda q, d: tabs[2, q, d]

    def to_other(start, tiles, places, source, dx, dy):
        def one(i, carry):
            to_x, to_y = place(gx, gy, dx, lax.div(i, 2), dy, lax.rem(i, 2))
            base = start + i * CAP
            fill(base, tiles, places, to_x * N_GY + to_y)
            send(base, CAP, source, (other, to_x, to_y))
            return carry

        lax.fori_loop(0, 4, one, 0)

    def to_same(start, dx, dy):
        first = 1 if dx == 0 and dy == 0 else 0

        def one(i, carry):
            to_x, to_y = place(gx, gy, dx, i, dy, 0)
            base = start + (i - first) * SELF
            d = to_x * N_GY + to_y
            fill(base + lax.rem(gy, 2) * CAP, near, near_places, d)
            fill(base + (1 - lax.rem(gy, 2)) * CAP, across, across_places, d)
            send(base, SELF, gx * N_GY + gy_pair, (comp, to_x, to_y))
            return carry

        lax.fori_loop(first, 2, one, 0)

    def keep():
        for tiles, places, source in ((near, near_places, gy), (across, across_places, gy_twin)):
            for q in range(CAP):
                arrived[(gx * N_GY + source) * CAP + q] = tiles[places(q, me)]

    for side in range(4):
        halo_copy(0, side).start()
    for i in range(1, 4):
        gather_table(i).start()
    for i in range(4):
        gather(i).start()
    for n, (dx, dy) in enumerate(STRAIGHT):
        to_other(n * 4 * CAP, ex, own_places, me, dx, dy)

    def pick(l):
        r = lax.broadcasted_iota(jnp.int32, (2 * LEV, TILE), 0)
        c = lax.broadcasted_iota(jnp.int32, (2 * LEV, TILE), 1)
        hit = ((r == l) & (c == 0)) | ((r == LEV + l) & (c == TILE - 1))
        return jnp.where(hit, 1.0, 0.0).astype(BF16)

    def send_halo(turn):
        for side in range(4):
            halo_copy(turn, side).start()

    def take_halo(turn, t):
        for side in range(4):
            halo_copy(turn, side).wait_recv()
        flat = t.reshape(LEV * PADDED, TILE)
        rows = [halo_in[turn, side].astype(F32) for side in range(4)]
        flat[pl.ds(TOP + ROWS, LEV, stride=PADDED), :] = jnp.where(gx < N_GX - 1, rows[0], 0.0)
        flat[pl.ds(TOP - 1, LEV, stride=PADDED), :] = jnp.where(gx > 0, rows[1], 0.0)
        last = jnp.where(gy < N_GY - 1, rows[2], 0.0)
        first = jnp.where(gy > 0, rows[3], 0.0)
        return jnp.transpose(jnp.concatenate([first, last], axis=0)).astype(BF16)

    def advance(t, edges, put):
        lane = lax.broadcasted_iota(jnp.int32, (ROWS, TILE), 1)

        def level(l, carry):
            mid = t[l, interior, :]
            above, below = t[l, pl.ds(TOP - 1, ROWS), :], t[l, pl.ds(TOP + 1, ROWS), :]
            sides = jnp.dot(edges, pick(l), preferred_element_type=F32)
            before = jnp.where(lane == 0, sides, pltpu.roll(mid, 1, 1))
            after = jnp.where(lane == TILE - 1, sides, pltpu.roll(mid, TILE - 1, 1))
            spread = above + below + before + after - 4.0 * mid
            carried = 0.5 * (
                vel[0, l].astype(F32) * (below - above) + vel[1, l].astype(F32) * (after - before)
            )
            put(l, mid + wet[...] * (diff[0, l] * spread - carried))
            return carry

        lax.fori_loop(0, LEV, level, 0)

    def put_tb(l, value):
        tb[l, interior, :] = value

    def put_tracer(l, value):
        tracer[l] = value

    for copy in small[3:]:
        copy.wait()
    row_wet = jnp.where(comp == 0, jnp.ones((1, TILE), F32), land_row[...].astype(F32))
    wet[...] = jnp.transpose(jnp.broadcast_to(row_wet, (ROWS, TILE)))
    edges = take_halo(0, ta)
    get_vel.wait()
    advance(ta, edges, put_tb)
    make_halo(1, tb)
    send_halo(1)

    for i in range(1, 4):
        gather_table(i).wait_recv()
    tabs_copy = pltpu.make_async_copy(tab_in, tabs, sem_tabs)
    tabs_copy.start()
    tabs_copy.wait()
    for i in range(4):
        gather(i).wait_recv()

    x_source, y_source = far(gx) * N_GY + gy, gx * N_GY + far(gy)
    four = 4 * CAP
    base = 2 * four

    def far_both(start):
        @pl.when(lax.rem(gx, 2) == 0)
        def _():
            to_other(start, far_x, far_x_places, x_source, 0, 2)

        @pl.when(lax.rem(gx, 2) == 1)
        def _():
            to_other(start, far_y, far_y_places, y_source, 2, 0)

    steps = []
    for n, (dx, dy) in enumerate(VIA_Z):
        if n < len(NEAR):
            steps.append((four, lambda at, k=NEAR[n]: to_other(at, far_x, far_x_places, x_source, 0, k)))
            steps.append((four, lambda at, k=NEAR[n]: to_other(at, far_y, far_y_places, y_source, k, 0)))
        elif n == len(NEAR):
            steps.append((four, far_both))
        steps.append((2 * SELF if dx or dy else SELF, lambda at, dx=dx, dy=dy: to_same(at, dx, dy)))
    for count, step in steps:
        step(base)
        base += count
    keep()

    def turn_w(i, carry):
        for j in range(TURNED):
            for k in range(K):
                w_out[i * TURNED + j, k] = jnp.transpose(w_out[i * TURNED + j, k])
        return carry

    for i in range(W_PARTS):
        get_w(i).wait()
    lax.fori_loop(0, ROWS // TURNED, turn_w, 0)
    edges = take_halo(1, tb)
    advance(tb, edges, put_tracer)

    for f in range(FLD):
        for l in range(LEV):
            spread[f, l : l + 1, :] = jnp.full((1, TILE), ip[f, l], F32)
    for turn in range(2):
        for side in range(4):
            halo_copy(turn, side).wait_send()
    for i in range(1, 4):
        gather_table(i).wait_send()
    for i in range(4):
        gather(i).wait_send()
    pltpu.make_async_copy(buf, buf, sem_send).wait()
    others = arrived.at[pl.ds(0, GROUP * CAP - SELF)]
    pltpu.make_async_copy(others, others, sem_recv).wait()


def remap_kernel(recv, land, w, arrived, tracer, spread, new_hbm, imp_hbm, new, imp, sem_out):
    comp = lax.axis_index("comp")
    tracer_rows = tracer.reshape(LEV * ROWS, TILE)
    new_rows = new.reshape(LEV * ROWS, TILE)
    copies = []
    for x in range(ROWS):
        wet = jnp.where(comp == 0, 1.0, land[0, x].astype(F32))
        source = jnp.concatenate([arrived[recv[k, x]] for k in range(K)], axis=1)
        weights = jnp.concatenate([w[x, k] for k in range(K)], axis=0)
        got = (jnp.dot(source, weights, preferred_element_type=F32) * wet).astype(BF16)
        imp[x] = got
        got = got.astype(F32)
        force = spread[0] * got[0:1, :]
        for f in range(1, FLD):
            force += spread[f] * got[f : f + 1, :]
        rows = pl.ds(x, LEV, stride=ROWS)
        new_rows[rows, :] = tracer_rows[rows, :] + wet * force
        if x % OUT_ROWS == OUT_ROWS - 1:
            i = x // OUT_ROWS
            done = pl.ds(i * OUT_ROWS, OUT_ROWS)
            copies.append(pltpu.make_async_copy(new.at[:, done], new_hbm.at[:, done], sem_out.at[0, i]))
            copies.append(pltpu.make_async_copy(imp.at[done], imp_hbm.at[done], sem_out.at[1, i]))
            copies[-2].start()
            copies[-1].start()
    for copy in copies:
        copy.wait()


ANY = pl.BlockSpec(memory_space=pl.ANY)
HBM = pl.BlockSpec(memory_space=pltpu.HBM)
VMEM = pl.BlockSpec(memory_space=pltpu.VMEM)
SMEM = pl.BlockSpec(memory_space=pltpu.SMEM)


def kept_in(space, arrays):
    return [pltpu.with_memory_space_constraint(a, space) for a in arrays]


def exchange(*arrays):
    dma = pltpu.SemaphoreType.DMA
    return pl.pallas_call(
        exchange_kernel,
        name="exchange",
        out_shape=(
            pltpu.VMEM((GROUP * CAP, FLD, TILE), BF16),
            pltpu.VMEM((LEV, ROWS, TILE), F32),
            pltpu.VMEM((ROWS, K, TILE, TILE), BF16),
            pltpu.VMEM((FLD, LEV, TILE), F32),
            pltpu.SMEM((K, ROWS), jnp.int32),
            pltpu.SMEM((1, ROWS), jnp.int32),
        ),
        in_specs=[HBM] * 9,
        out_specs=(VMEM, VMEM, VMEM, VMEM, SMEM, SMEM),
        scratch_shapes=[
            pltpu.VMEM((LEV, PADDED, TILE), F32),
            pltpu.VMEM((LEV, PADDED, TILE), F32),
            pltpu.VMEM((2, LEV, ROWS, TILE), BF16),
            *[pltpu.VMEM((ROWS, FLD, TILE), BF16) for _ in range(5)],
            pltpu.VMEM((3, CAP, GROUP), jnp.int32),
            pltpu.VMEM((GROUP * CAP - SELF, FLD, TILE), BF16),
            pltpu.VMEM((2, 4, LEV, TILE), BF16),
            pltpu.VMEM((2, 4, LEV, TILE), BF16),
            pltpu.VMEM((2, LEV, TILE), F32),
            pltpu.VMEM((ROWS, TILE), F32),
            pltpu.VMEM((FLD, LEV), F32),
            pltpu.VMEM((1, ROWS), jnp.int32),
            pltpu.SMEM((1, LEV), F32),
            pltpu.SMEM((2, CAP, GROUP), jnp.int32),
            pltpu.SMEM((3, CAP, GROUP), jnp.int32),
            pltpu.SMEM((FLD, LEV), F32),
            dma((S_PARTS,)),
            dma,
            dma((7,)),
            dma((W_PARTS,)),
            dma,
            dma,
            dma((2, 4)),
            dma((2, 4)),
            dma((4,)),
            dma((4,)),
            dma((3,)),
            dma((3,)),
            dma,
        ],
        compiler_params=pltpu.CompilerParams(collective_id=0, has_side_effects=True, vmem_limit_bytes=16 << 20),
    )(*kept_in(pltpu.HBM, arrays))


def remap(recv, land, weights, arrived, tracer, spread):
    return pl.pallas_call(
        remap_kernel,
        name="remap",
        out_shape=(
            jax.ShapeDtypeStruct((LEV, ROWS, TILE), F32),
            jax.ShapeDtypeStruct((ROWS, FLD, TILE), BF16),
        ),
        in_specs=[SMEM, SMEM, VMEM, VMEM, VMEM, VMEM],
        out_specs=(ANY, ANY),
        scratch_shapes=[
            pltpu.VMEM((LEV, ROWS, TILE), F32),
            pltpu.VMEM((ROWS, FLD, TILE), BF16),
            pltpu.SemaphoreType.DMA((2, ROWS // OUT_ROWS)),
        ],
        compiler_params=pltpu.CompilerParams(vmem_limit_bytes=16 << 20),
    )(*kept_in(pltpu.SMEM, (recv, land)), *kept_in(pltpu.VMEM, (weights, arrived, tracer, spread)))


def per_device(
    state, velocity, diffusivity, export_proj, import_proj, intersection_weights, recv_slots, send_slots, land
):
    land = land.reshape(1, ROWS)
    table = send_slots[:, 0, 0].transpose(0, 2, 1)
    recv = recv_slots[0, :, 0].T
    arrived, tracer, weights, spread, recv, land = exchange(
        state[0], velocity[0], intersection_weights[0, :, 0], export_proj[0], diffusivity, table, land, recv,
        import_proj[0].T,
    )
    new_state, imported = remap(recv, land, weights, arrived, tracer, spread)
    return new_state[None], imported[None]


def solution(mesh):
    return jax.shard_map(
        per_device,
        mesh=mesh,
        in_specs=(
            P("comp", None, "gx", "gy"),
            P("comp", None, None, "gx", "gy"),
            P("comp", None),
            P("comp", None, None),
            P("comp", None, None),
            P("comp", "gx", "gy", None, None, None),
            P("comp", "gx", "gy", None),
            P(None, "gx", "gy", None, None),
            P("gx", "gy"),
        ),
        out_specs=(P("comp", None, "gx", "gy"), P("comp", "gx", None, "gy")),
        check_vma=False,
    )
```

```python
import jax
import jax.numpy as jnp
from jax import lax
from jax.experimental import pallas as pl
from jax.experimental.pallas import tpu as pltpu
from jax.sharding import PartitionSpec as P

MESH = pl.DeviceIdType.MESH
F32 = jnp.float32
BF16 = jnp.bfloat16

LEV, FLD, K = 16, 8, 4
ROWS, TILE = 128, 128
N_GX, N_GY = 8, 8
GROUP, CAP = 64, 16
TOP = 8
PADDED = ROWS + 2 * TOP
W_PARTS = 8
S_PARTS = 4
OUT_ROWS = 8
TURNED = 4
SELF = 2 * CAP
EACH = tuple((core, high) for core in range(2) for high in range(2))
STRAIGHT = ((1, 1), (3, 3))
VIA_Z = ((1, 3), (3, 1), (0, 1), (1, 0), (0, 3), (3, 0), (0, 0))
NEAR = (0, 1, 3)


def place(gx, gy, dx, core, dy, high):
    to_x = lax.rem(lax.div(gx, 2) + dx, 4) * 2 + lax.rem(gx + core, 2)
    to_y = lax.rem(lax.div(gy, 2) + dy, 4) * 2 + lax.rem(gy + high, 2)
    return to_x, to_y


def exchange_kernel(
    state_hbm, vel_hbm, w_hbm, proj_hbm, diff_hbm, table_hbm, land_hbm, recv_hbm, ip_hbm,
    arrived, tracer, w_out, spread, recv_out, land_out,
    ta, tb, vel, ex, near, across, far_x, far_y, tab_in, buf,
    halo_out, halo_in, edge, wet, proj, land_row, diff, table, tabs, ip,
    sem_state, sem_vel, sem_small, sem_w, sem_send, sem_recv, sem_hs, sem_hr,
    sem_gs, sem_gr, sem_ts, sem_tr, sem_tabs,
):
    comp, gx, gy = lax.axis_index("comp"), lax.axis_index("gx"), lax.axis_index("gy")
    other = 1 - comp
    me = gx * N_GY + gy
    up, down = lax.rem(gx + N_GX - 1, N_GX), lax.rem(gx + 1, N_GX)
    left, right = lax.rem(gy + N_GY - 1, N_GY), lax.rem(gy + 1, N_GY)
    beside = ((comp, up, gy), (comp, down, gy), (comp, gx, left), (comp, gx, right))

    small = [
        pltpu.make_async_copy(source, target, sem_small.at[i])
        for i, (source, target) in enumerate(
            (
                (proj_hbm, proj),
                (land_hbm, land_out),
                (table_hbm, table),
                (land_hbm, land_row),
                (diff_hbm, diff),
                (recv_hbm, recv_out),
                (ip_hbm, ip),
            )
        )
    ]
    interior = pl.ds(TOP, ROWS)
    slab = ROWS // S_PARTS

    def get_state(i):
        return pltpu.make_async_copy(
            state_hbm.at[:, pl.ds(i * slab, slab)], ta.at[:, pl.ds(TOP + i * slab, slab)], sem_state.at[i]
        )

    for i in range(S_PARTS):
        get_state(i).start()
    barrier = pltpu.get_barrier_semaphore()
    peers = [(other, *place(gx, gy, dx, core, dy, high)) for dx, dy in STRAIGHT for core, high in EACH]
    peers += [(other, *place(gx, gy, 0, core, dy, high)) for dy in range(4) for core, high in EACH]
    peers += [(other, *place(gx, gy, dx, core, 0, high)) for dx in range(1, 4) for core, high in EACH]
    peers += [(comp, *place(gx, gy, dx, core, dy, 0)) for dx, dy in VIA_Z for core in range(2) if dx or dy or core]
    peers += [(comp, *place(gx, gy, 2, 0, 0, 0)), (comp, *place(gx, gy, 0, 0, 2, 0)), *beside]
    for device in peers:
        pl.semaphore_signal(barrier, inc=1, device_id=device, device_id_type=MESH)
    for copy in small:
        copy.start()
    get_vel = pltpu.make_async_copy(vel_hbm, vel, sem_vel)
    get_vel.start()

    part = w_hbm.shape[0] // W_PARTS

    def get_w(i):
        rows = pl.ds(i * part, part)
        return pltpu.make_async_copy(w_hbm.at[rows], w_out.at[rows], sem_w.at[i])

    for i in range(W_PARTS):
        get_w(i).start()

    for copy in small[:3]:
        copy.wait()
    columns = [jnp.broadcast_to(proj[:, l : l + 1], (FLD, TILE)) for l in range(LEV)]

    def export(i, carry):
        for j in range(8):
            x = i * 8 + j
            total = columns[0] * ta[0, pl.ds(TOP + x, 1), :]
            for l in range(1, LEV):
                total += columns[l] * ta[l, pl.ds(TOP + x, 1), :]
            ex[x] = (total * jnp.where(comp == 0, 1.0, land_out[0, x].astype(F32))).astype(BF16)
        return carry

    for i in range(S_PARTS):
        get_state(i).wait()
        lax.fori_loop(i * slab // 8, (i + 1) * slab // 8, export, 0)
    r = lax.broadcasted_iota(jnp.int32, (FLD, TILE), 0)
    c = lax.broadcasted_iota(jnp.int32, (FLD, TILE), 1)
    both_ends = jnp.where(((r == 0) & (c == 0)) | ((r == 1) & (c == TILE - 1)), 1.0, 0.0).astype(BF16)

    def halo_copy(turn, side):
        return pltpu.make_async_remote_copy(
            src_ref=halo_out.at[turn, side],
            dst_ref=halo_in.at[turn, side],
            send_sem=sem_hs.at[turn, side],
            recv_sem=sem_hr.at[turn, side],
            device_id=beside[side],
            device_id_type=MESH,
        )

    def make_halo(turn, t):
        flat = t.reshape(LEV * PADDED, TILE)
        halo_out[turn, 0] = flat[pl.ds(TOP, LEV, stride=PADDED), :].astype(BF16)
        halo_out[turn, 1] = flat[pl.ds(TOP + ROWS - 1, LEV, stride=PADDED), :].astype(BF16)

        for l in range(LEV):
            ends = lax.dot_general(
                both_ends, t[l, interior, :].astype(BF16), (((1,), (1,)), ((), ())), preferred_element_type=F32
            )
            edge[0, l : l + 1, :] = ends[0:1]
            edge[1, l : l + 1, :] = ends[1:2]
        halo_out[turn, 2] = edge[0].astype(BF16)
        halo_out[turn, 3] = edge[1].astype(BF16)

    make_halo(0, ta)
    pl.semaphore_wait(barrier, len(peers))

    far = lambda g: lax.rem(g + 4, 8)
    gy_pair = lax.div(gy, 2) * 2
    gy_twin = gy_pair + 1 - lax.rem(gy, 2)
    relays = ((other, gx, gy), (other, gx, gy_twin), (comp, far(gx), gy), (comp, gx, far(gy)))
    taken = (near, across, far_x, far_y)

    def gather(i):
        return pltpu.make_async_remote_copy(
            src_ref=ex, dst_ref=taken[i], send_sem=sem_gs.at[i], recv_sem=sem_gr.at[i],
            device_id=relays[i], device_id_type=MESH,
        )

    def gather_table(i):
        return pltpu.make_async_remote_copy(
            src_ref=table_hbm.at[comp], dst_ref=tab_in.at[i - 1], send_sem=sem_ts.at[i - 1], recv_sem=sem_tr.at[i - 1],
            device_id=relays[i], device_id_type=MESH,
        )

    def fill(base, tiles, places, d):
        for q in range(CAP):
            buf[base + q] = tiles[places(q, d)]

    def send(base, count, source, device):
        pltpu.make_async_remote_copy(
            src_ref=buf.at[pl.ds(base, count)],
            dst_ref=arrived.at[pl.ds(source * CAP, count)],
            send_sem=sem_send,
            recv_sem=sem_recv,
            device_id=device,
            device_id_type=MESH,
        ).start()

    own_places = lambda q, d: table[comp, q, d]
    near_places = lambda q, d: table[other, q, d]
    across_places = lambda q, d: tabs[0, q, d]
    far_x_places = lambda q, d: tabs[1, q, d]
    far_y_places = lambda q, d: tabs[2, q, d]

    def to_other(start, tiles, places, source, dx, dy):
        def one(i, carry):
            to_x, to_y = place(gx, gy, dx, lax.div(i, 2), dy, lax.rem(i, 2))
            base = start + i * CAP
            fill(base, tiles, places, to_x * N_GY + to_y)
            send(base, CAP, source, (other, to_x, to_y))
            return carry

        lax.fori_loop(0, 4, one, 0)

    def to_same(start, dx, dy):
        first = 1 if dx == 0 and dy == 0 else 0

        def one(i, carry):
            to_x, to_y = place(gx, gy, dx, i, dy, 0)
            base = start + (i - first) * SELF
            d = to_x * N_GY + to_y
            fill(base + lax.rem(gy, 2) * CAP, near, near_places, d)
            fill(base + (1 - lax.rem(gy, 2)) * CAP, across, across_places, d)
            send(base, SELF, gx * N_GY + gy_pair, (comp, to_x, to_y))
            return carry

        lax.fori_loop(first, 2, one, 0)

    def keep():
        for tiles, places, source in ((near, near_places, gy), (across, across_places, gy_twin)):
            for q in range(CAP):
                arrived[(gx * N_GY + source) * CAP + q] = tiles[places(q, me)]

    for side in range(4):
        halo_copy(0, side).start()
    for i in range(1, 4):
        gather_table(i).start()
    for i in range(4):
        gather(i).start()
    for n, (dx, dy) in enumerate(STRAIGHT):
        to_other(n * 4 * CAP, ex, own_places, me, dx, dy)

    def pick(l):
        r = lax.broadcasted_iota(jnp.int32, (2 * LEV, TILE), 0)
        c = lax.broadcasted_iota(jnp.int32, (2 * LEV, TILE), 1)
        hit = ((r == l) & (c == 0)) | ((r == LEV + l) & (c == TILE - 1))
        return jnp.where(hit, 1.0, 0.0).astype(BF16)

    def send_halo(turn):
        for side in range(4):
            halo_copy(turn, side).start()

    def take_halo(turn, t):
        for side in range(4):
            halo_copy(turn, side).wait_recv()
        flat = t.reshape(LEV * PADDED, TILE)
        rows = [halo_in[turn, side].astype(F32) for side in range(4)]
        flat[pl.ds(TOP + ROWS, LEV, stride=PADDED), :] = jnp.where(gx < N_GX - 1, rows[0], 0.0)
        flat[pl.ds(TOP - 1, LEV, stride=PADDED), :] = jnp.where(gx > 0, rows[1], 0.0)
        last = jnp.where(gy < N_GY - 1, rows[2], 0.0)
        first = jnp.where(gy > 0, rows[3], 0.0)
        return jnp.transpose(jnp.concatenate([first, last], axis=0)).astype(BF16)

    def advance(t, edges, put):
        lane = lax.broadcasted_iota(jnp.int32, (ROWS, TILE), 1)

        def level(l, carry):
            mid = t[l, interior, :]
            above, below = t[l, pl.ds(TOP - 1, ROWS), :], t[l, pl.ds(TOP + 1, ROWS), :]
            sides = jnp.dot(edges, pick(l), preferred_element_type=F32)
            before = jnp.where(lane == 0, sides, pltpu.roll(mid, 1, 1))
            after = jnp.where(lane == TILE - 1, sides, pltpu.roll(mid, TILE - 1, 1))
            spread = above + below + before + after - 4.0 * mid
            carried = 0.5 * (
                vel[0, l].astype(F32) * (below - above) + vel[1, l].astype(F32) * (after - before)
            )
            put(l, mid + wet[...] * (diff[0, l] * spread - carried))
            return carry

        lax.fori_loop(0, LEV, level, 0)

    def put_tb(l, value):
        tb[l, interior, :] = value

    def put_tracer(l, value):
        tracer[l] = value

    for copy in small[3:]:
        copy.wait()
    row_wet = jnp.where(comp == 0, jnp.ones((1, TILE), F32), land_row[...].astype(F32))
    wet[...] = jnp.transpose(jnp.broadcast_to(row_wet, (ROWS, TILE)))
    edges = take_halo(0, ta)
    get_vel.wait()
    advance(ta, edges, put_tb)
    make_halo(1, tb)
    send_halo(1)

    for i in range(1, 4):
        gather_table(i).wait_recv()
    tabs_copy = pltpu.make_async_copy(tab_in, tabs, sem_tabs)
    tabs_copy.start()
    tabs_copy.wait()
    x_source, y_source = far(gx) * N_GY + gy, gx * N_GY + far(gy)
    four = 4 * CAP
    base = 2 * four

    def far_both(start):
        @pl.when(lax.rem(gx, 2) == 0)
        def _():
            to_other(start, far_x, far_x_places, x_source, 0, 2)

        @pl.when(lax.rem(gx, 2) == 1)
        def _():
            to_other(start, far_y, far_y_places, y_source, 2, 0)

    via_x = [(four, lambda at, k=k: to_other(at, far_x, far_x_places, x_source, 0, k)) for k in NEAR]
    via_y = [(four, lambda at, k=k: to_other(at, far_y, far_y_places, y_source, k, 0)) for k in NEAR]
    via_z = [
        (2 * SELF if dx or dy else SELF, lambda at, dx=dx, dy=dy: to_same(at, dx, dy)) for dx, dy in VIA_Z
    ]
    both = [(four, far_both)]
    rest = [via_x[1], via_y[1], via_x[2], via_y[2], *both, via_x[0], via_y[0]]
    steps = [step for pair in zip(via_z, rest) for step in pair]
    for n, (count, step) in enumerate(steps):
        for i in {0: (0, 1), 1: (2,), 3: (3,)}.get(n, ()):
            gather(i).wait_recv()
        step(base)
        base += count
    keep()

    def turn_w(i, carry):
        for j in range(TURNED):
            for k in range(K):
                w_out[i * TURNED + j, k] = jnp.transpose(w_out[i * TURNED + j, k])
        return carry

    for i in range(W_PARTS):
        get_w(i).wait()
    lax.fori_loop(0, ROWS // TURNED, turn_w, 0)
    edges = take_halo(1, tb)
    advance(tb, edges, put_tracer)

    for f in range(FLD):
        for l in range(LEV):
            spread[f, l : l + 1, :] = jnp.full((1, TILE), ip[f, l], F32)
    for turn in range(2):
        for side in range(4):
            halo_copy(turn, side).wait_send()
    for i in range(1, 4):
        gather_table(i).wait_send()
    for i in range(4):
        gather(i).wait_send()
    pltpu.make_async_copy(buf, buf, sem_send).wait()
    others = arrived.at[pl.ds(0, GROUP * CAP - SELF)]
    pltpu.make_async_copy(others, others, sem_recv).wait()


def remap_kernel(recv, land, w, arrived, tracer, spread, new_hbm, imp_hbm, new, imp, sem_out):
    comp = lax.axis_index("comp")
    tracer_rows = tracer.reshape(LEV * ROWS, TILE)
    new_rows = new.reshape(LEV * ROWS, TILE)
    copies = []
    for x in range(ROWS):
        wet = jnp.where(comp == 0, 1.0, land[0, x].astype(F32))
        source = jnp.concatenate([arrived[recv[k, x]] for k in range(K)], axis=1)
        weights = jnp.concatenate([w[x, k] for k in range(K)], axis=0)
        got = (jnp.dot(source, weights, preferred_element_type=F32) * wet).astype(BF16)
        imp[x] = got
        got = got.astype(F32)
        force = spread[0] * got[0:1, :]
        for f in range(1, FLD):
            force += spread[f] * got[f : f + 1, :]
        rows = pl.ds(x, LEV, stride=ROWS)
        new_rows[rows, :] = tracer_rows[rows, :] + wet * force
        if x % OUT_ROWS == OUT_ROWS - 1:
            i = x // OUT_ROWS
            done = pl.ds(i * OUT_ROWS, OUT_ROWS)
            copies.append(pltpu.make_async_copy(new.at[:, done], new_hbm.at[:, done], sem_out.at[0, i]))
            copies.append(pltpu.make_async_copy(imp.at[done], imp_hbm.at[done], sem_out.at[1, i]))
            copies[-2].start()
            copies[-1].start()
    for copy in copies:
        copy.wait()


ANY = pl.BlockSpec(memory_space=pl.ANY)
HBM = pl.BlockSpec(memory_space=pltpu.HBM)
VMEM = pl.BlockSpec(memory_space=pltpu.VMEM)
SMEM = pl.BlockSpec(memory_space=pltpu.SMEM)


def kept_in(space, arrays):
    return [pltpu.with_memory_space_constraint(a, space) for a in arrays]


def exchange(*arrays):
    dma = pltpu.SemaphoreType.DMA
    return pl.pallas_call(
        exchange_kernel,
        name="exchange",
        out_shape=(
            pltpu.VMEM((GROUP * CAP, FLD, TILE), BF16),
            pltpu.VMEM((LEV, ROWS, TILE), F32),
            pltpu.VMEM((ROWS, K, TILE, TILE), BF16),
            pltpu.VMEM((FLD, LEV, TILE), F32),
            pltpu.SMEM((K, ROWS), jnp.int32),
            pltpu.SMEM((1, ROWS), jnp.int32),
        ),
        in_specs=[HBM] * 9,
        out_specs=(VMEM, VMEM, VMEM, VMEM, SMEM, SMEM),
        scratch_shapes=[
            pltpu.VMEM((LEV, PADDED, TILE), F32),
            pltpu.VMEM((LEV, PADDED, TILE), F32),
            pltpu.VMEM((2, LEV, ROWS, TILE), BF16),
            *[pltpu.VMEM((ROWS, FLD, TILE), BF16) for _ in range(5)],
            pltpu.VMEM((3, CAP, GROUP), jnp.int32),
            pltpu.VMEM((GROUP * CAP - SELF, FLD, TILE), BF16),
            pltpu.VMEM((2, 4, LEV, TILE), BF16),
            pltpu.VMEM((2, 4, LEV, TILE), BF16),
            pltpu.VMEM((2, LEV, TILE), F32),
            pltpu.VMEM((ROWS, TILE), F32),
            pltpu.VMEM((FLD, LEV), F32),
            pltpu.VMEM((1, ROWS), jnp.int32),
            pltpu.SMEM((1, LEV), F32),
            pltpu.SMEM((2, CAP, GROUP), jnp.int32),
            pltpu.SMEM((3, CAP, GROUP), jnp.int32),
            pltpu.SMEM((FLD, LEV), F32),
            dma((S_PARTS,)),
            dma,
            dma((7,)),
            dma((W_PARTS,)),
            dma,
            dma,
            dma((2, 4)),
            dma((2, 4)),
            dma((4,)),
            dma((4,)),
            dma((3,)),
            dma((3,)),
            dma,
        ],
        compiler_params=pltpu.CompilerParams(collective_id=0, has_side_effects=True, vmem_limit_bytes=16 << 20),
    )(*kept_in(pltpu.HBM, arrays))


def remap(recv, land, weights, arrived, tracer, spread):
    return pl.pallas_call(
        remap_kernel,
        name="remap",
        out_shape=(
            jax.ShapeDtypeStruct((LEV, ROWS, TILE), F32),
            jax.ShapeDtypeStruct((ROWS, FLD, TILE), BF16),
        ),
        in_specs=[SMEM, SMEM, VMEM, VMEM, VMEM, VMEM],
        out_specs=(ANY, ANY),
        scratch_shapes=[
            pltpu.VMEM((LEV, ROWS, TILE), F32),
            pltpu.VMEM((ROWS, FLD, TILE), BF16),
            pltpu.SemaphoreType.DMA((2, ROWS // OUT_ROWS)),
        ],
        compiler_params=pltpu.CompilerParams(vmem_limit_bytes=16 << 20),
    )(*kept_in(pltpu.SMEM, (recv, land)), *kept_in(pltpu.VMEM, (weights, arrived, tracer, spread)))


def per_device(
    state, velocity, diffusivity, export_proj, import_proj, intersection_weights, recv_slots, send_slots, land
):
    land = land.reshape(1, ROWS)
    table = send_slots[:, 0, 0].transpose(0, 2, 1)
    recv = recv_slots[0, :, 0].T
    arrived, tracer, weights, spread, recv, land = exchange(
        state[0], velocity[0], intersection_weights[0, :, 0], export_proj[0], diffusivity, table, land, recv,
        import_proj[0].T,
    )
    new_state, imported = remap(recv, land, weights, arrived, tracer, spread)
    return new_state[None], imported[None]


def solution(mesh):
    return jax.shard_map(
        per_device,
        mesh=mesh,
        in_specs=(
            P("comp", None, "gx", "gy"),
            P("comp", None, None, "gx", "gy"),
            P("comp", None),
            P("comp", None, None),
            P("comp", None, None),
            P("comp", "gx", "gy", None, None, None),
            P("comp", "gx", "gy", None),
            P(None, "gx", "gy", None, None),
            P("gx", "gy"),
        ),
        out_specs=(P("comp", None, "gx", "gy"), P("comp", "gx", None, "gy")),
        check_vma=False,
    )
```

```python
import jax
import jax.numpy as jnp
from jax import lax
from jax.experimental import pallas as pl
from jax.experimental.pallas import tpu as pltpu
from jax.sharding import PartitionSpec as P

MESH = pl.DeviceIdType.MESH
F32 = jnp.float32
BF16 = jnp.bfloat16

LEV, FLD, K = 16, 8, 4
ROWS, TILE = 128, 128
N_GX, N_GY = 8, 8
GROUP, CAP = 64, 16
TOP = 8
PADDED = ROWS + 2 * TOP
W_PARTS = 8
S_PARTS = 4
OUT_ROWS = 8
TURNED = 4
SELF = 2 * CAP
EACH = tuple((core, high) for core in range(2) for high in range(2))
STRAIGHT = ((1, 1), (3, 3))
VIA_Z = ((1, 3), (3, 1), (0, 1), (1, 0), (0, 3), (3, 0), (0, 0))
NEAR = (0, 1, 3)


def place(gx, gy, dx, core, dy, high):
    to_x = lax.rem(lax.div(gx, 2) + dx, 4) * 2 + lax.rem(gx + core, 2)
    to_y = lax.rem(lax.div(gy, 2) + dy, 4) * 2 + lax.rem(gy + high, 2)
    return to_x, to_y


def exchange_kernel(
    state_hbm, vel_hbm, w_hbm, proj_hbm, diff_hbm, table_hbm, land_hbm, recv_hbm, ip_hbm,
    arrived, tracer, w_out, spread, recv_out, land_out,
    ta, tb, vel, ex, near, across, far_x, far_y, tab_in, buf,
    halo_out, halo_in, edge, wet, proj, land_row, diff, table, tabs, ip,
    sem_state, sem_vel, sem_small, sem_w, sem_send, sem_recv, sem_hs, sem_hr,
    sem_gs, sem_gr, sem_ts, sem_tr, sem_tabs,
):
    comp, gx, gy = lax.axis_index("comp"), lax.axis_index("gx"), lax.axis_index("gy")
    other = 1 - comp
    me = gx * N_GY + gy
    up, down = lax.rem(gx + N_GX - 1, N_GX), lax.rem(gx + 1, N_GX)
    left, right = lax.rem(gy + N_GY - 1, N_GY), lax.rem(gy + 1, N_GY)
    beside = ((comp, up, gy), (comp, down, gy), (comp, gx, left), (comp, gx, right))

    small = [
        pltpu.make_async_copy(source, target, sem_small.at[i])
        for i, (source, target) in enumerate(
            (
                (proj_hbm, proj),
                (land_hbm, land_out),
                (table_hbm, table),
                (land_hbm, land_row),
                (diff_hbm, diff),
                (recv_hbm, recv_out),
                (ip_hbm, ip),
            )
        )
    ]
    interior = pl.ds(TOP, ROWS)
    slab = ROWS // S_PARTS

    def get_state(i):
        return pltpu.make_async_copy(
            state_hbm.at[:, pl.ds(i * slab, slab)], ta.at[:, pl.ds(TOP + i * slab, slab)], sem_state.at[i]
        )

    for i in range(S_PARTS):
        get_state(i).start()
    barrier = pltpu.get_barrier_semaphore()
    peers = [(other, *place(gx, gy, dx, core, dy, high)) for dx, dy in STRAIGHT for core, high in EACH]
    peers += [(other, *place(gx, gy, 0, core, dy, high)) for dy in range(4) for core, high in EACH]
    peers += [(other, *place(gx, gy, dx, core, 0, high)) for dx in range(1, 4) for core, high in EACH]
    peers += [(comp, *place(gx, gy, dx, core, dy, 0)) for dx, dy in VIA_Z for core in range(2) if dx or dy or core]
    peers += [(comp, *place(gx, gy, 2, 0, 0, 0)), (comp, *place(gx, gy, 0, 0, 2, 0)), *beside]
    for device in peers:
        pl.semaphore_signal(barrier, inc=1, device_id=device, device_id_type=MESH)
    for copy in small:
        copy.start()
    get_vel = pltpu.make_async_copy(vel_hbm, vel, sem_vel)
    get_vel.start()

    part = w_hbm.shape[0] // W_PARTS

    def get_w(i):
        rows = pl.ds(i * part, part)
        return pltpu.make_async_copy(w_hbm.at[rows], w_out.at[rows], sem_w.at[i])

    for i in range(W_PARTS):
        get_w(i).start()

    for copy in small[:3]:
        copy.wait()
    columns = [jnp.broadcast_to(proj[:, l : l + 1], (FLD, TILE)) for l in range(LEV)]

    def export(i, carry):
        for j in range(8):
            x = i * 8 + j
            total = columns[0] * ta[0, pl.ds(TOP + x, 1), :]
            for l in range(1, LEV):
                total += columns[l] * ta[l, pl.ds(TOP + x, 1), :]
            ex[x] = (total * jnp.where(comp == 0, 1.0, land_out[0, x].astype(F32))).astype(BF16)
        return carry

    for i in range(S_PARTS):
        get_state(i).wait()
        lax.fori_loop(i * slab // 8, (i + 1) * slab // 8, export, 0)
    r = lax.broadcasted_iota(jnp.int32, (FLD, TILE), 0)
    c = lax.broadcasted_iota(jnp.int32, (FLD, TILE), 1)
    both_ends = jnp.where(((r == 0) & (c == 0)) | ((r == 1) & (c == TILE - 1)), 1.0, 0.0).astype(BF16)

    def halo_copy(turn, side):
        return pltpu.make_async_remote_copy(
            src_ref=halo_out.at[turn, side],
            dst_ref=halo_in.at[turn, side],
            send_sem=sem_hs.at[turn, side],
            recv_sem=sem_hr.at[turn, side],
            device_id=beside[side],
            device_id_type=MESH,
        )

    def make_halo(turn, t):
        flat = t.reshape(LEV * PADDED, TILE)
        halo_out[turn, 0] = flat[pl.ds(TOP, LEV, stride=PADDED), :].astype(BF16)
        halo_out[turn, 1] = flat[pl.ds(TOP + ROWS - 1, LEV, stride=PADDED), :].astype(BF16)

        for l in range(LEV):
            ends = lax.dot_general(
                both_ends, t[l, interior, :].astype(BF16), (((1,), (1,)), ((), ())), preferred_element_type=F32
            )
            edge[0, l : l + 1, :] = ends[0:1]
            edge[1, l : l + 1, :] = ends[1:2]
        halo_out[turn, 2] = edge[0].astype(BF16)
        halo_out[turn, 3] = edge[1].astype(BF16)

    make_halo(0, ta)
    pl.semaphore_wait(barrier, len(peers))

    far = lambda g: lax.rem(g + 4, 8)
    gy_pair = lax.div(gy, 2) * 2
    gy_twin = gy_pair + 1 - lax.rem(gy, 2)
    relays = ((other, gx, gy), (other, gx, gy_twin), (comp, far(gx), gy), (comp, gx, far(gy)))
    taken = (near, across, far_x, far_y)

    def gather(i):
        return pltpu.make_async_remote_copy(
            src_ref=ex, dst_ref=taken[i], send_sem=sem_gs.at[i], recv_sem=sem_gr.at[i],
            device_id=relays[i], device_id_type=MESH,
        )

    def gather_table(i):
        return pltpu.make_async_remote_copy(
            src_ref=table_hbm.at[comp], dst_ref=tab_in.at[i - 1], send_sem=sem_ts.at[i - 1], recv_sem=sem_tr.at[i - 1],
            device_id=relays[i], device_id_type=MESH,
        )

    def fill(base, tiles, places, d):
        for q in range(CAP):
            buf[base + q] = tiles[places(q, d)]

    def send(base, count, source, device):
        pltpu.make_async_remote_copy(
            src_ref=buf.at[pl.ds(base, count)],
            dst_ref=arrived.at[pl.ds(source * CAP, count)],
            send_sem=sem_send,
            recv_sem=sem_recv,
            device_id=device,
            device_id_type=MESH,
        ).start()

    own_places = lambda q, d: table[comp, q, d]
    near_places = lambda q, d: table[other, q, d]
    across_places = lambda q, d: tabs[0, q, d]
    far_x_places = lambda q, d: tabs[1, q, d]
    far_y_places = lambda q, d: tabs[2, q, d]

    def to_other(start, tiles, places, source, dx, dy):
        def one(i, carry):
            to_x, to_y = place(gx, gy, dx, lax.div(i, 2), dy, lax.rem(i, 2))
            base = start + i * CAP
            fill(base, tiles, places, to_x * N_GY + to_y)
            send(base, CAP, source, (other, to_x, to_y))
            return carry

        lax.fori_loop(0, 4, one, 0)

    def to_same(start, dx, dy):
        first = 1 if dx == 0 and dy == 0 else 0

        def one(i, carry):
            to_x, to_y = place(gx, gy, dx, i, dy, 0)
            base = start + (i - first) * SELF
            d = to_x * N_GY + to_y
            fill(base + lax.rem(gy, 2) * CAP, near, near_places, d)
            fill(base + (1 - lax.rem(gy, 2)) * CAP, across, across_places, d)
            send(base, SELF, gx * N_GY + gy_pair, (comp, to_x, to_y))
            return carry

        lax.fori_loop(first, 2, one, 0)

    def keep():
        for tiles, places, source in ((near, near_places, gy), (across, across_places, gy_twin)):
            for q in range(CAP):
                arrived[(gx * N_GY + source) * CAP + q] = tiles[places(q, me)]

    for side in range(4):
        halo_copy(0, side).start()
    for i in range(1, 4):
        gather_table(i).start()
    for i in (2, 3, 0, 1):
        gather(i).start()
    for n, (dx, dy) in enumerate(STRAIGHT):
        to_other(n * 4 * CAP, ex, own_places, me, dx, dy)

    def pick(l):
        r = lax.broadcasted_iota(jnp.int32, (2 * LEV, TILE), 0)
        c = lax.broadcasted_iota(jnp.int32, (2 * LEV, TILE), 1)
        hit = ((r == l) & (c == 0)) | ((r == LEV + l) & (c == TILE - 1))
        return jnp.where(hit, 1.0, 0.0).astype(BF16)

    def send_halo(turn):
        for side in range(4):
            halo_copy(turn, side).start()

    def take_halo(turn, t):
        for side in range(4):
            halo_copy(turn, side).wait_recv()
        flat = t.reshape(LEV * PADDED, TILE)
        rows = [halo_in[turn, side].astype(F32) for side in range(4)]
        flat[pl.ds(TOP + ROWS, LEV, stride=PADDED), :] = jnp.where(gx < N_GX - 1, rows[0], 0.0)
        flat[pl.ds(TOP - 1, LEV, stride=PADDED), :] = jnp.where(gx > 0, rows[1], 0.0)
        last = jnp.where(gy < N_GY - 1, rows[2], 0.0)
        first = jnp.where(gy > 0, rows[3], 0.0)
        return jnp.transpose(jnp.concatenate([first, last], axis=0)).astype(BF16)

    def advance(t, edges, put):
        lane = lax.broadcasted_iota(jnp.int32, (ROWS, TILE), 1)

        def level(l, carry):
            mid = t[l, interior, :]
            above, below = t[l, pl.ds(TOP - 1, ROWS), :], t[l, pl.ds(TOP + 1, ROWS), :]
            sides = jnp.dot(edges, pick(l), preferred_element_type=F32)
            before = jnp.where(lane == 0, sides, pltpu.roll(mid, 1, 1))
            after = jnp.where(lane == TILE - 1, sides, pltpu.roll(mid, TILE - 1, 1))
            spread = above + below + before + after - 4.0 * mid
            carried = 0.5 * (
                vel[0, l].astype(F32) * (below - above) + vel[1, l].astype(F32) * (after - before)
            )
            put(l, mid + wet[...] * (diff[0, l] * spread - carried))
            return carry

        lax.fori_loop(0, LEV, level, 0)

    def put_tb(l, value):
        tb[l, interior, :] = value

    def put_tracer(l, value):
        tracer[l] = value

    for copy in small[3:]:
        copy.wait()
    row_wet = jnp.where(comp == 0, jnp.ones((1, TILE), F32), land_row[...].astype(F32))
    wet[...] = jnp.transpose(jnp.broadcast_to(row_wet, (ROWS, TILE)))
    edges = take_halo(0, ta)
    get_vel.wait()
    advance(ta, edges, put_tb)
    make_halo(1, tb)
    send_halo(1)

    for i in range(1, 4):
        gather_table(i).wait_recv()
    tabs_copy = pltpu.make_async_copy(tab_in, tabs, sem_tabs)
    tabs_copy.start()
    tabs_copy.wait()
    x_source, y_source = far(gx) * N_GY + gy, gx * N_GY + far(gy)
    four = 4 * CAP
    base = 2 * four

    def far_both(start):
        @pl.when(lax.rem(gx, 2) == 0)
        def _():
            to_other(start, far_x, far_x_places, x_source, 0, 2)

        @pl.when(lax.rem(gx, 2) == 1)
        def _():
            to_other(start, far_y, far_y_places, y_source, 2, 0)

    via_x = [(four, lambda at, k=k: to_other(at, far_x, far_x_places, x_source, 0, k)) for k in NEAR]
    via_y = [(four, lambda at, k=k: to_other(at, far_y, far_y_places, y_source, k, 0)) for k in NEAR]
    via_z = [
        (2 * SELF if dx or dy else SELF, lambda at, dx=dx, dy=dy: to_same(at, dx, dy)) for dx, dy in VIA_Z
    ]
    both = [(four, far_both)]
    rest = [via_x[1], via_y[1], via_x[2], via_y[2], *both, via_x[0], via_y[0]]
    steps = [step for pair in zip(via_z, rest) for step in pair]
    for n, (count, step) in enumerate(steps):
        for i in {0: (0, 1), 1: (2,), 3: (3,)}.get(n, ()):
            gather(i).wait_recv()
        step(base)
        base += count
    keep()

    def turn_w(i, carry):
        for j in range(TURNED):
            for k in range(K):
                w_out[i * TURNED + j, k] = jnp.transpose(w_out[i * TURNED + j, k])
        return carry

    for i in range(W_PARTS):
        get_w(i).wait()
    lax.fori_loop(0, ROWS // TURNED, turn_w, 0)
    edges = take_halo(1, tb)
    advance(tb, edges, put_tracer)

    for f in range(FLD):
        for l in range(LEV):
            spread[f, l : l + 1, :] = jnp.full((1, TILE), ip[f, l], F32)
    for turn in range(2):
        for side in range(4):
            halo_copy(turn, side).wait_send()
    for i in range(1, 4):
        gather_table(i).wait_send()
    for i in range(4):
        gather(i).wait_send()
    pltpu.make_async_copy(buf, buf, sem_send).wait()
    others = arrived.at[pl.ds(0, GROUP * CAP - SELF)]
    pltpu.make_async_copy(others, others, sem_recv).wait()


def remap_kernel(recv, land, w, arrived, tracer, spread, new_hbm, imp_hbm, new, imp, sem_out):
    comp = lax.axis_index("comp")
    tracer_rows = tracer.reshape(LEV * ROWS, TILE)
    new_rows = new.reshape(LEV * ROWS, TILE)
    copies = []
    for x in range(ROWS):
        wet = jnp.where(comp == 0, 1.0, land[0, x].astype(F32))
        source = jnp.concatenate([arrived[recv[k, x]] for k in range(K)], axis=1)
        weights = jnp.concatenate([w[x, k] for k in range(K)], axis=0)
        got = (jnp.dot(source, weights, preferred_element_type=F32) * wet).astype(BF16)
        imp[x] = got
        got = got.astype(F32)
        force = spread[0] * got[0:1, :]
        for f in range(1, FLD):
            force += spread[f] * got[f : f + 1, :]
        rows = pl.ds(x, LEV, stride=ROWS)
        new_rows[rows, :] = tracer_rows[rows, :] + wet * force
        if x % OUT_ROWS == OUT_ROWS - 1:
            i = x // OUT_ROWS
            done = pl.ds(i * OUT_ROWS, OUT_ROWS)
            copies.append(pltpu.make_async_copy(new.at[:, done], new_hbm.at[:, done], sem_out.at[0, i]))
            copies.append(pltpu.make_async_copy(imp.at[done], imp_hbm.at[done], sem_out.at[1, i]))
            copies[-2].start()
            copies[-1].start()
    for copy in copies:
        copy.wait()


ANY = pl.BlockSpec(memory_space=pl.ANY)
HBM = pl.BlockSpec(memory_space=pltpu.HBM)
VMEM = pl.BlockSpec(memory_space=pltpu.VMEM)
SMEM = pl.BlockSpec(memory_space=pltpu.SMEM)


def kept_in(space, arrays):
    return [pltpu.with_memory_space_constraint(a, space) for a in arrays]


def exchange(*arrays):
    dma = pltpu.SemaphoreType.DMA
    return pl.pallas_call(
        exchange_kernel,
        name="exchange",
        out_shape=(
            pltpu.VMEM((GROUP * CAP, FLD, TILE), BF16),
            pltpu.VMEM((LEV, ROWS, TILE), F32),
            pltpu.VMEM((ROWS, K, TILE, TILE), BF16),
            pltpu.VMEM((FLD, LEV, TILE), F32),
            pltpu.SMEM((K, ROWS), jnp.int32),
            pltpu.SMEM((1, ROWS), jnp.int32),
        ),
        in_specs=[HBM] * 9,
        out_specs=(VMEM, VMEM, VMEM, VMEM, SMEM, SMEM),
        scratch_shapes=[
            pltpu.VMEM((LEV, PADDED, TILE), F32),
            pltpu.VMEM((LEV, PADDED, TILE), F32),
            pltpu.VMEM((2, LEV, ROWS, TILE), BF16),
            *[pltpu.VMEM((ROWS, FLD, TILE), BF16) for _ in range(5)],
            pltpu.VMEM((3, CAP, GROUP), jnp.int32),
            pltpu.VMEM((GROUP * CAP - SELF, FLD, TILE), BF16),
            pltpu.VMEM((2, 4, LEV, TILE), BF16),
            pltpu.VMEM((2, 4, LEV, TILE), BF16),
            pltpu.VMEM((2, LEV, TILE), F32),
            pltpu.VMEM((ROWS, TILE), F32),
            pltpu.VMEM((FLD, LEV), F32),
            pltpu.VMEM((1, ROWS), jnp.int32),
            pltpu.SMEM((1, LEV), F32),
            pltpu.SMEM((2, CAP, GROUP), jnp.int32),
            pltpu.SMEM((3, CAP, GROUP), jnp.int32),
            pltpu.SMEM((FLD, LEV), F32),
            dma((S_PARTS,)),
            dma,
            dma((7,)),
            dma((W_PARTS,)),
            dma,
            dma,
            dma((2, 4)),
            dma((2, 4)),
            dma((4,)),
            dma((4,)),
            dma((3,)),
            dma((3,)),
            dma,
        ],
        compiler_params=pltpu.CompilerParams(collective_id=0, has_side_effects=True, vmem_limit_bytes=16 << 20),
    )(*kept_in(pltpu.HBM, arrays))


def remap(recv, land, weights, arrived, tracer, spread):
    return pl.pallas_call(
        remap_kernel,
        name="remap",
        out_shape=(
            jax.ShapeDtypeStruct((LEV, ROWS, TILE), F32),
            jax.ShapeDtypeStruct((ROWS, FLD, TILE), BF16),
        ),
        in_specs=[SMEM, SMEM, VMEM, VMEM, VMEM, VMEM],
        out_specs=(ANY, ANY),
        scratch_shapes=[
            pltpu.VMEM((LEV, ROWS, TILE), F32),
            pltpu.VMEM((ROWS, FLD, TILE), BF16),
            pltpu.SemaphoreType.DMA((2, ROWS // OUT_ROWS)),
        ],
        compiler_params=pltpu.CompilerParams(vmem_limit_bytes=16 << 20),
    )(*kept_in(pltpu.SMEM, (recv, land)), *kept_in(pltpu.VMEM, (weights, arrived, tracer, spread)))


def per_device(
    state, velocity, diffusivity, export_proj, import_proj, intersection_weights, recv_slots, send_slots, land
):
    land = land.reshape(1, ROWS)
    table = send_slots[:, 0, 0].transpose(0, 2, 1)
    recv = recv_slots[0, :, 0].T
    arrived, tracer, weights, spread, recv, land = exchange(
        state[0], velocity[0], intersection_weights[0, :, 0], export_proj[0], diffusivity, table, land, recv,
        import_proj[0].T,
    )
    new_state, imported = remap(recv, land, weights, arrived, tracer, spread)
    return new_state[None], imported[None]


def solution(mesh):
    return jax.shard_map(
        per_device,
        mesh=mesh,
        in_specs=(
            P("comp", None, "gx", "gy"),
            P("comp", None, None, "gx", "gy"),
            P("comp", None),
            P("comp", None, None),
            P("comp", None, None),
            P("comp", "gx", "gy", None, None, None),
            P("comp", "gx", "gy", None),
            P(None, "gx", "gy", None, None),
            P("gx", "gy"),
        ),
        out_specs=(P("comp", None, "gx", "gy"), P("comp", "gx", None, "gy")),
        check_vma=False,
    )
```
